32 devices in a mesh: group: 2 (over y), store: 4 (over z), tensor: 2 (over x), rep: 2 (over core).
Axes of the slice: x: 2, y: 2, z: 4, core: 2. Of those that a mesh axis runs over, the one named last changes fastest.
Arguments:
- queries: bfloat16 [8, 256, 4096], P(('group', 'store'), 'rep', 'tensor'), parts along dimension 0, may hold values from -40 to 40
- hidden: bfloat16 [8, 256, 7168], P(('group', 'store'), 'rep', 'tensor'), parts along dimension 0, may hold values from -6 to 6
- key_value_weight: bfloat16 [7168, 1024], P(('tensor', 'rep')), may hold values from -0.0625 to 0.0625
- page_store: bfloat16 [256, 2, 128, 512], P(('group', 'store'), None, None, 'tensor'), parts along dimension 0, may hold values from -30 to 30
- prefix_holder: int32 [8, 64, 1], P('group'), parts along dimension 0, may hold values from 0 to 3; in each aligned block of 32 rows (0 to 31, 32 to 63, ..., all dimensions but the last counted through in order) at most 8 rows name the same one
- prefix_slot: int32 [8, 64], P('group'), parts along dimension 0, may hold values from 0 to 31
- prefix_len: int32 [8], P('group'), parts along dimension 0, may hold values from 1 to 8192, 26214 in all
- new_owner: int32 [2, 8], P(None, 'group'), parts along dimension 1, may hold values from 0 to 3, each once within a row
Outputs:
- attended: bfloat16 [8, 256, 4096], P(('group', 'store'), 'rep', 'tensor'), parts along dimension 0
- added_pages: bfloat16 [8, 2, 2, 128, 512], P(('group', 'store'), 'rep', None, None, 'tensor'), parts along dimension 0
The draws below stay inside these ranges and needn't reach their ends.
There are 2 independent parts, one for each index of `group`. The reference program is written for one: setup_inputs(seed, part) draws one part's arguments, and reference() takes and returns one part's arrays. A program takes and returns all parts, laid end to end along the dimension named above; an argument that names none is the same for every part. Nothing has to cross between parts.
Inputs may be any that keep to these rules, and one draw needn't show every extreme that they name: `prefix_holder`: within each half of one request's list (32 entries in order) no holder is named more than 8 times. The entry names row prefix_holder * 32 + prefix_slot of the group's page store. `new_owner`: each row is a permutation of the store indices.
All inputs are finite; a program needn't handle non-finite values.
Results may differ from the reference program's by a relative error of at most 0.02.
Values may be sent and summed in bfloat16 or wider, within the bound.
A program may use at most 128 MiB of HBM per device.

```python
import math
import jax
import jax.numpy as jnp
import numpy as np
from jax import lax

MODEL_WIDTH = 7168
QUERY_HEADS = 32
KEY_VALUE_HEADS = 4
HEAD_ENTRIES = 128
PAGE_TOKENS = 128
PREFIX_PAGE_MAX = 64
PAGES_DEV = 32
HOLD_CAP = 8
GROUP_REQUESTS = 4
REQUEST_TOKENS = 256
GROUP_STORE_PAGE = 128
N_STORE = 4
N_REP = 2


def draw_queries(key, part):
    key = jax.random.fold_in(key, 31)
    sample_draw = jnp.clip(2.5 * jax.random.normal(key, (GROUP_REQUESTS, REQUEST_TOKENS, KEY_VALUE_HEADS, QUERY_HEADS // KEY_VALUE_HEADS, HEAD_ENTRIES), jnp.float32), -10.0, 10.0)
    return jnp.clip(sample_draw, -40.0, 40.0).reshape(GROUP_REQUESTS, REQUEST_TOKENS, QUERY_HEADS * HEAD_ENTRIES).astype(jnp.bfloat16)


def draw_page_store(key, part):
    key = jax.random.fold_in(key, 47)
    sample_draw = jnp.clip(jax.random.normal(key, (GROUP_STORE_PAGE, 2, PAGE_TOKENS, KEY_VALUE_HEADS, HEAD_ENTRIES), jnp.float32), -4.5, 4.5)
    return jnp.clip(sample_draw, -30.0, 30.0).reshape(GROUP_STORE_PAGE, 2, PAGE_TOKENS, KEY_VALUE_HEADS * HEAD_ENTRIES).astype(jnp.bfloat16)


def plant(values, key, low, largest):
    place = [jax.random.randint(jax.random.fold_in(key, axis), (), 0, length) for axis, length in enumerate(values.shape)]
    widest = values.shape.index(max(values.shape))
    neighbour = place[:widest] + [(place[widest] + 1) % values.shape[widest]] + place[widest + 1:]
    return values.at[tuple(place)].set(low).at[tuple(neighbour)].set(largest)


def block_levels(stream_key, dims, shards, smallest, top_value):
    def one(dim, blocks):
        heights = jax.random.uniform(jax.random.fold_in(jax.random.fold_in(stream_key, 6), dim), (blocks,), jnp.float32, smallest / len(shards), top_value / len(shards))
        return jnp.repeat(jnp.exp(heights), dims[dim] // blocks).reshape((-1,) + (1,) * (len(dims) - dim - 1))

    level = one(*shards[0])
    for cut in shards[1:]:
        level = level * one(*cut)
    return level


def profile(amount, total, most, lean):
    portions = [(1 << 20) // math.isqrt(standing ** lean) + 1 for standing in range(2, amount + 1)]
    rest, holding = total - most - (amount - 1), [1] * (amount - 1)
    while rest > 0:
        candidates = [i for i in range(amount - 1) if holding[i] < most]
        mass, left = sum([portions[i] for i in candidates]), rest
        for i in candidates:
            extra = min(most - holding[i], max(1, left * portions[i] // mass), rest)
            holding[i] = holding[i] + extra
            rest = rest - extra
    return np.array([most] + holding)


def uneven_parts(key, number_of, total, reach, lean):
    if number_of == 2:
        one = jax.random.randint(key, (), max(1, total - reach), min(reach, total - 1) + 1)
        return jnp.stack([one, total - one])
    tallies = jnp.asarray(profile(number_of, total, reach, lean), jnp.int32)
    pairs = (number_of - 1) // 2
    giver, taker = tallies[1:1 + 2 * pairs:2], tallies[2:2 + 2 * pairs:2]
    room = jnp.minimum(giver - 1, reach - taker)
    moved = jax.random.randint(jax.random.fold_in(key, 1), (pairs,), 0, 1 << 20) % (room + 1)
    tallies = tallies.at[1:1 + 2 * pairs:2].set(giver - moved).at[2:2 + 2 * pairs:2].set(taker + moved)
    return tallies[jax.random.permutation(jax.random.fold_in(key, 2), number_of)]


def shared_out(rng, own, number, rows, number_of, top, bound, slope):
    ranking = jax.random.permutation(rng, number_of)
    packed, usual = shares(number_of, rows * top, bound, slope, True), shares(number_of, rows * top, bound, slope, False)
    places = jnp.arange(number_of)

    def named(sizes, offset_by):
        used = int((sizes > 0).sum())
        fixed = max(1, used // 4)
        moved = fixed + (places - fixed + offset_by * (used - fixed)) % max(1, number_of - fixed)
        return jnp.zeros((number_of,), jnp.int32).at[ranking[jnp.where(places < fixed, places, moved)]].set(jnp.asarray(sizes, jnp.int32))

    sizes = jnp.where(number % 4 == 0, named(packed, number // 4), named(usual, number - number // 4 - 1))
    mixed = jax.random.permutation(jax.random.fold_in(own, 3), number_of)
    source_of, taker = mixed[0:number_of // 2 * 2:2], mixed[1:number_of // 2 * 2:2]
    slack = jnp.minimum(sizes[source_of] - 1, bound - sizes[taker]) // 2
    slack = jnp.where((source_of == ranking[0]) | (taker == ranking[0]) | (sizes[taker] == 0), 0, jnp.maximum(slack, 0))
    moved = jax.random.randint(jax.random.fold_in(own, 4), (number_of // 2,), 0, 1 << 20) % (slack + 1)
    sizes = sizes.at[source_of].add(-moved).at[taker].add(moved)
    items = jnp.searchsorted(jnp.cumsum(sizes), jnp.arange(rows * top), side="right").astype(jnp.int32)
    grid = items.reshape(top, rows).T
    grid = grid[jax.random.permutation(jax.random.fold_in(own, 1), rows)]
    offset_by = jax.random.randint(jax.random.fold_in(own, 2), (rows, 1), 0, top)
    return jnp.take_along_axis(grid, (jnp.arange(top)[None, :] + offset_by) % top, axis=1)


def shares(amount, total, reach, slope, full):
    weights = [(1 << 20) // math.isqrt(grade ** slope) + 1 for grade in range(1, amount + 1)]
    largest = reach if full else min(reach, max(-(-total // amount), total * weights[0] // sum(weights)))
    least = 1 if total - largest >= amount - 1 else 0
    counts, rest = [largest] + [least] * (amount - 1), total - largest - least * (amount - 1)
    while rest > 0:
        candidates = [i for i in range(1, amount) if counts[i] < largest] or [i for i in range(1, amount) if counts[i] < reach]
        whole, left = sum([weights[i] for i in candidates]), rest
        for i in candidates:
            more = min(reach - counts[i], max(1, left * weights[i] // whole), rest)
            counts[i] = counts[i] + more
            rest = rest - more
    return np.array(counts)


def gaussian(rng, dims, width, most, cuts=(), held_as=jnp.bfloat16):
    factor_of = block_levels(rng, dims, cuts, -0.22, 0.18) if cuts else 1.0
    values = jax.random.normal(rng, dims, jnp.float32) * width * factor_of
    return jnp.minimum(jnp.maximum(values, -most), most).astype(held_as)


def setup_inputs(seed: int = 0, part: int = 0) -> dict:
    streams_of = jax.random.split(jax.random.key(seed), 9)
    part_keys = jax.random.split(jax.random.fold_in(streams_of[8], part), 9)
    queries = draw_queries(jax.random.fold_in(jax.random.fold_in(streams_of[8], part), 71), part)
    hidden = gaussian(part_keys[1], (GROUP_REQUESTS, REQUEST_TOKENS, MODEL_WIDTH), 1.0, 6.0, ((0, 4), (1, 2), (2, 2)))
    key_value_weight = gaussian(streams_of[2], (MODEL_WIDTH, 2 * KEY_VALUE_HEADS * HEAD_ENTRIES), MODEL_WIDTH ** -0.5, 0.0625, ((0, 4),))
    page_store = draw_page_store(jax.random.fold_in(jax.random.fold_in(streams_of[8], part), 71), part)
    prefix_holder_keys = jax.random.split(jax.random.fold_in(part_keys[4], 1), GROUP_REQUESTS * PREFIX_PAGE_MAX // (PREFIX_PAGE_MAX // 2))
    prefix_holder_turns = jax.random.permutation(jax.random.fold_in(part_keys[4], 3), GROUP_REQUESTS * PREFIX_PAGE_MAX // (PREFIX_PAGE_MAX // 2))
    prefix_holder = jax.vmap(lambda own, number: shared_out(jax.random.fold_in(part_keys[4], 2), own, number, PREFIX_PAGE_MAX // 2, N_STORE, 1, HOLD_CAP, 0))(prefix_holder_keys, prefix_holder_turns).reshape((GROUP_REQUESTS, PREFIX_PAGE_MAX, 1))
    prefix_slot = plant(jax.random.randint(part_keys[5], (GROUP_REQUESTS, PREFIX_PAGE_MAX), 0, PAGES_DEV), jax.random.fold_in(part_keys[5], 1), 0, PAGES_DEV - 1).astype(jnp.int32)
    prefix_len = uneven_parts(part_keys[6], GROUP_REQUESTS, GROUP_REQUESTS * PREFIX_PAGE_MAX * PAGE_TOKENS * 4 // 5, PREFIX_PAGE_MAX * PAGE_TOKENS, 2).astype(jnp.int32)
    new_owner = jax.vmap(lambda own: jax.random.permutation(own, GROUP_REQUESTS))(jax.random.split(part_keys[7], N_REP)).reshape((N_REP, GROUP_REQUESTS)).astype(jnp.int32)
    return {"queries": queries, "hidden": hidden, "key_value_weight": key_value_weight, "page_store": page_store, "prefix_holder": prefix_holder, "prefix_slot": prefix_slot, "prefix_len": prefix_len, "new_owner": new_owner}


NEG_FILL = -1e+30

def reference(queries, hidden, key_value_weight, page_store, prefix_holder, prefix_slot, prefix_len, new_owner):
    serving_groups = QUERY_HEADS // KEY_VALUE_HEADS
    score_scale = 1.0 / math.sqrt(HEAD_ENTRIES)
    key_value_pair = jnp.einsum('scd,dk->sck', hidden.astype(jnp.float32), key_value_weight.astype(jnp.float32), precision=lax.Precision.HIGHEST).astype(jnp.bfloat16)
    recent_pages = key_value_pair.reshape(GROUP_REQUESTS, N_REP, PAGE_TOKENS, KEY_VALUE_HEADS, 2, HEAD_ENTRIES).transpose(0, 1, 4, 2, 3, 5).reshape(GROUP_REQUESTS, N_REP, 2, PAGE_TOKENS, KEY_VALUE_HEADS * HEAD_ENTRIES)
    page_owners = jnp.transpose(new_owner).astype(jnp.int32)
    split_halves = jnp.broadcast_to(jnp.arange(N_REP, dtype=jnp.int32)[None, :], (GROUP_REQUESTS, N_REP))
    added_pages = jnp.zeros((GROUP_REQUESTS, N_REP, 2, PAGE_TOKENS, KEY_VALUE_HEADS * HEAD_ENTRIES), jnp.bfloat16).at[page_owners, split_halves].set(recent_pages)
    page_ids = (prefix_holder[:, :, 0] * PAGES_DEV + prefix_slot).astype(jnp.int32)
    token_pos = jnp.arange(PREFIX_PAGE_MAX * PAGE_TOKENS, dtype=jnp.int32)
    causal = jnp.arange(REQUEST_TOKENS, dtype=jnp.int32)[None, :] <= jnp.arange(REQUEST_TOKENS, dtype=jnp.int32)[:, None]

    def one_request(inputs):
        query_matrix, local_block, row_ids, length = inputs
        cached_prefix = page_store[row_ids]
        prefix_keys = cached_prefix[:, 0].reshape(PREFIX_PAGE_MAX * PAGE_TOKENS, KEY_VALUE_HEADS, HEAD_ENTRIES).astype(jnp.float32)
        prefix_values = cached_prefix[:, 1].reshape(PREFIX_PAGE_MAX * PAGE_TOKENS, KEY_VALUE_HEADS, HEAD_ENTRIES).astype(jnp.float32)
        local_split = local_block.reshape(REQUEST_TOKENS, KEY_VALUE_HEADS, 2, HEAD_ENTRIES).astype(jnp.float32)
        keys_new = local_split[:, :, 0]
        values_new = local_split[:, :, 1]
        query_float = query_matrix.reshape(REQUEST_TOKENS, KEY_VALUE_HEADS, serving_groups, HEAD_ENTRIES).astype(jnp.float32)
        score_pre = jnp.einsum('thgd,khd->hgtk', query_float, prefix_keys, precision=lax.Precision.HIGHEST) * score_scale
        score_new = jnp.einsum('thgd,khd->hgtk', query_float, keys_new, precision=lax.Precision.HIGHEST) * score_scale
        valid_pre = (token_pos < length)[None, None, None, :]
        valid_new = causal[None, None]
        row_max = jnp.maximum(lax.optimization_barrier(jnp.max(jnp.where(valid_pre, score_pre, NEG_FILL), axis=-1)), lax.optimization_barrier(jnp.max(jnp.where(valid_new, score_new, NEG_FILL), axis=-1)))
        exp_pre = jnp.where(valid_pre, jnp.exp(score_pre - row_max[..., None]), 0.0)
        exp_new = jnp.where(valid_new, jnp.exp(score_new - row_max[..., None]), 0.0)
        weight_sum = lax.optimization_barrier(jnp.sum(exp_pre, axis=-1)) + lax.optimization_barrier(jnp.sum(exp_new, axis=-1))
        rounded_pre = lax.optimization_barrier(exp_pre.astype(jnp.bfloat16)).astype(jnp.float32)
        rounded_new = lax.optimization_barrier(exp_new.astype(jnp.bfloat16)).astype(jnp.float32)
        weighted = jnp.einsum('hgtk,khd->hgtd', rounded_pre, prefix_values, precision=lax.Precision.HIGHEST)
        weighted = weighted + jnp.einsum('hgtk,khd->hgtd', rounded_new, values_new, precision=lax.Precision.HIGHEST)
        result = weighted / weight_sum[..., None]
        return result.transpose(2, 0, 1, 3).reshape(REQUEST_TOKENS, QUERY_HEADS * HEAD_ENTRIES).astype(jnp.bfloat16)
    attended = lax.map(one_request, (queries, key_value_pair, page_ids, prefix_len))
    return (attended, added_pages)
```

```python
import functools
import math

import jax
import jax.numpy as jnp
from jax import lax
from jax.experimental import pallas as pl
from jax.experimental.pallas import tpu as pltpu
from jax.sharding import PartitionSpec as P

HEAD_ENTRIES = 128


NEG_FILL = -1e30


def from_behind(block, axis, distance):
    devices = range(lax.axis_size(axis))
    route = [(i - distance, i) for i in devices if i - distance in devices]
    return lax.ppermute(block, axis, route)


def attend_block(running, query_matrix, key_rows, values, allowed):
    row_max, weight_sum, weighted = running
    score_scale = 1.0 / math.sqrt(key_rows.shape[-1])
    scores = (
        jnp.einsum("rhgd,khd->hgrk", query_matrix, key_rows, preferred_element_type=jnp.float32)
        * score_scale
    )
    scores = jnp.where(allowed, scores, NEG_FILL)
    fresh_max = jnp.maximum(row_max, jnp.max(scores, axis=-1))
    shrink = jnp.exp(row_max - fresh_max)
    weights = jnp.where(allowed, jnp.exp(scores - fresh_max[..., None]), 0.0)
    weight_sum = weight_sum * shrink + jnp.sum(weights, axis=-1)
    weighted = weighted * shrink[..., None] + jnp.einsum(
        "hgrk,khd->hgrd", weights.astype(jnp.bfloat16), values, preferred_element_type=jnp.float32
    )
    return (fresh_max, weight_sum, weighted)


def start_carry(kv_heads, serving_groups, row_count, head_size):
    return (
        jnp.full((kv_heads, serving_groups, row_count), NEG_FILL, jnp.float32),
        jnp.zeros((kv_heads, serving_groups, row_count), jnp.float32),
        jnp.zeros((kv_heads, serving_groups, row_count, head_size), jnp.float32),
    )


def scan_pages(running, query_matrix, pulled, token_ok):
    page_count = pulled.shape[0]
    page_len = pulled.shape[2]
    kv_heads = query_matrix.shape[1]
    head_size = query_matrix.shape[3]
    per_block = math.gcd(page_count, max(1, 1024 // page_len))
    blocks = page_count // per_block
    page_blocks = pulled.reshape(blocks, per_block, 2, page_len, kv_heads, head_size)
    ok_blocks = token_ok.reshape(blocks, per_block * page_len)

    def visit_block(state_now, block_item):
        page_block, block_ok = block_item
        key_rows = page_block[:, 0].reshape(per_block * page_len, kv_heads, head_size)
        values = page_block[:, 1].reshape(per_block * page_len, kv_heads, head_size)
        return (
            attend_block(state_now, query_matrix, key_rows, values, block_ok[None, None, None, :]),
            None,
        )

    running, unused = lax.scan(visit_block, running, (page_blocks, ok_blocks))
    return running


def pull_plan(holders, places):
    member = (holders[:, :, None] == jnp.arange(places, dtype=jnp.int32)[None, None, :]).astype(
        jnp.int32
    )
    ranking = jnp.sum((jnp.cumsum(member, axis=1) - 1) * member, axis=-1)
    return (holders, ranking)


def send_pages(page_store, holders_part, ranking, slots, capacity, store_id):
    chosen = (holders_part == store_id)[:, None, :] & (
        ranking[:, None, :] == jnp.arange(capacity, dtype=jnp.int32)[None, :, None]
    )
    slot_of = jnp.sum(jnp.where(chosen, slots[:, None, :], 0), axis=-1)
    return page_store[slot_of.reshape(-1)]


def receive_order(received, holders_part, ranking, store_id, capacity):
    own_holders = lax.dynamic_index_in_dim(holders_part, store_id, 0, keepdims=False)
    my_rank = lax.dynamic_index_in_dim(ranking, store_id, 0, keepdims=False)
    return received[own_holders * capacity + my_rank]


def pull_shards(
    queries, hidden, key_value_weight, page_store, prefix_holder, prefix_slot, prefix_len, new_owner
):
    store_id = lax.axis_index("store")
    rep_id = lax.axis_index("rep")
    stores = lax.axis_size("store")
    tensors = lax.axis_size("tensor")
    tokens = queries.shape[1]
    page_len = page_store.shape[2]
    local_width = page_store.shape[3]
    kv_heads = local_width // HEAD_ENTRIES
    serving_groups = queries.shape[2] // local_width
    quarter_rows = hidden.shape[2]
    own_rows = hidden[0]
    weight_full = lax.all_gather(key_value_weight, "rep", axis=0, tiled=True)
    weight_five = weight_full.reshape(quarter_rows, tensors, kv_heads, 2, HEAD_ENTRIES)
    partial_value = jnp.einsum(
        "tc,cghkd->gkthd", own_rows, weight_five, preferred_element_type=jnp.float32
    )
    summed = lax.psum_scatter(
        partial_value.reshape(tensors * 2 * tokens, kv_heads * HEAD_ENTRIES).astype(jnp.bfloat16),
        "tensor",
        scatter_dimension=0,
        tiled=True,
    )
    own_kv = summed.reshape(2, tokens, kv_heads * HEAD_ENTRIES)
    spread = lax.all_gather(own_kv[None], "store", axis=0, tiled=True)
    owner_row = lax.dynamic_index_in_dim(new_owner, rep_id, 0, keepdims=False)
    owner_pick = (owner_row == store_id).astype(jnp.bfloat16)
    new_page = jnp.einsum(
        "n,nktc->ktc", owner_pick, spread, preferred_element_type=jnp.float32
    ).astype(jnp.bfloat16)
    added_pages = new_page.reshape(1, 1, 2, tokens, kv_heads * HEAD_ENTRIES)
    earlier = from_behind(own_kv, "rep", 1)
    new_keys = jnp.concatenate([earlier[0], own_kv[0]], 0).reshape(
        2 * tokens, kv_heads, HEAD_ENTRIES
    )
    new_values = jnp.concatenate([earlier[1], own_kv[1]], 0).reshape(
        2 * tokens, kv_heads, HEAD_ENTRIES
    )
    key_index = jnp.arange(2 * tokens, dtype=jnp.int32)[None, :]
    query_index = jnp.arange(tokens, dtype=jnp.int32)[:, None]
    allowed_new = jnp.where(key_index < tokens, rep_id > 0, key_index - tokens <= query_index)
    my_len = lax.dynamic_index_in_dim(prefix_len, store_id, 0, keepdims=False)
    list_len = prefix_slot.shape[1]
    holders = prefix_holder[:, :, 0]
    query_matrix = queries[0].reshape(tokens, kv_heads, serving_groups, HEAD_ENTRIES)
    capacity = 2 * max(2, list_len // (2 * stores))
    holders_part, ranking = pull_plan(holders, stores)
    outgoing = send_pages(page_store, holders_part, ranking, prefix_slot, capacity, store_id)
    incoming = lax.all_to_all(outgoing, "store", split_axis=0, concat_axis=0, tiled=True)
    pulled = receive_order(incoming, holders_part, ranking, store_id, capacity)
    token_ok = jnp.arange(list_len * page_len, dtype=jnp.int32) < my_len
    running = scan_pages(
        start_carry(kv_heads, serving_groups, tokens, HEAD_ENTRIES), query_matrix, pulled, token_ok
    )
    running = attend_block(running, query_matrix, new_keys, new_values, allowed_new[None, None])
    row_max, weight_sum, weighted = running
    result = (
        (weighted / weight_sum[..., None])
        .transpose(2, 0, 1, 3)
        .reshape(1, tokens, kv_heads * serving_groups * HEAD_ENTRIES)
    )
    return (result.astype(jnp.bfloat16), added_pages)


MESH = pl.DeviceIdType.MESH
SCORE_FACTOR = math.log2(math.e) / math.sqrt(HEAD_ENTRIES)
KERNEL_BYTES = 60 * 2**20


def held_table(holders, slots, lengths, capacity, page_len, store_id):
    count = holders.shape[1]
    place = jnp.arange(count, dtype=jnp.int32)
    same = (holders[:, :, None] == holders[:, None, :]) & (place[None, None, :] < place[None, :, None])
    ranking = jnp.sum(same.astype(jnp.int32), axis=-1)
    chosen = (holders == store_id)[:, None, :] & (
        ranking[:, None, :] == jnp.arange(capacity, dtype=jnp.int32)[None, :, None]
    )
    visible = jnp.clip(lengths[:, None] - place[None, :] * page_len, 0, page_len)
    slot_of = jnp.sum(jnp.where(chosen, slots[:, None, :], 0), axis=-1)
    visible_of = jnp.sum(jnp.where(chosen, visible[:, None, :], 0), axis=-1)
    return jnp.stack([slot_of, visible_of])


def merge(first, second):
    out1, max1, sum1 = first
    out2, max2, sum2 = second
    top = jnp.maximum(max1, max2)
    share1 = sum1 * jnp.exp2((max1 - top) * SCORE_FACTOR)
    share2 = sum2 * jnp.exp2((max2 - top) * SCORE_FACTOR)
    total = share1 + share2
    inverse = 1.0 / jnp.maximum(total, 1.0)
    return (out1 * (share1 * inverse) + out2 * (share2 * inverse), top, total)


def attend_kernel(
    stores, kv_heads, group_heads, capacity, tokens, page_len,
    table, q_ref, pages, new_kv, out_ref,
    q_buf, part, part_stat, inc, inc_stat, k_buf, v_buf,
    q_send, q_recv, p_send, p_recv, t_send, t_recv,
):
    me = lax.axis_index("store")
    rep_id = lax.axis_index("rep")
    has_left = me > 0
    has_right = me < stores - 1
    entries = HEAD_ENTRIES
    head_width = group_heads * entries

    def q_copy(s, h, side):
        step = 1 if side == 0 else -1
        return pltpu.make_async_remote_copy(
            src_ref=q_buf.at[s, h], dst_ref=q_buf.at[s, h],
            send_sem=q_send.at[side, s, h], recv_sem=q_recv.at[s, h],
            device_id={"store": me + step}, device_id_type=MESH,
        )

    def part_copies(s, h, side):
        step = 1 if side == 0 else -1
        return [
            pltpu.make_async_remote_copy(
                src_ref=source.at[s, h], dst_ref=target.at[side, s, h],
                send_sem=send.at[s, h], recv_sem=recv.at[side, s, h],
                device_id={"store": me + step}, device_id_type=MESH,
            )
            for source, target, send, recv in (
                (part, inc, p_send, p_recv), (part_stat, inc_stat, t_send, t_recv)
            )
        ]

    barrier = pltpu.get_barrier_semaphore()

    @pl.when(has_left)
    def _():
        pl.semaphore_signal(barrier, inc=1, device_id={"store": me - 1}, device_id_type=MESH)

    @pl.when(has_right)
    def _():
        pl.semaphore_signal(barrier, inc=1, device_id={"store": me + 1}, device_id_type=MESH)

    for h in range(kv_heads):
        q_buf[me, h] = q_ref[:, h * head_width:(h + 1) * head_width]

    pl.semaphore_wait(barrier, has_left.astype(jnp.int32) + has_right.astype(jnp.int32))

    def pass_query(s, h):
        @pl.when((s <= me) & has_right)
        def _():
            q_copy(s, h, 0).start()

        @pl.when((s >= me) & has_left)
        def _():
            q_copy(s, h, 1).start()

    for h in range(kv_heads):
        pass_query(me, h)

    lane = lax.broadcasted_iota(jnp.int32, (tokens, entries), 1)

    def softmax_block(scores, values):
        top = jnp.max(scores, axis=1, keepdims=True)
        weights = jnp.exp2((scores - top) * SCORE_FACTOR).astype(jnp.bfloat16)
        return top, jnp.dot(weights, values, preferred_element_type=jnp.float32)

    def compute(s, h):
        columns = pl.ds(pl.multiple_of(h * entries, entries), entries)
        spare = pages[table[0, s, 0], 0, 0:8, columns].astype(jnp.float32)[0:1]
        row = lax.broadcasted_iota(jnp.int32, (page_len, entries), 0)

        def lay(r, unused):
            slot = table[0, s, r]
            seen = row < table[1, s, r]
            place = pl.ds(pl.multiple_of(r * page_len, page_len), page_len)
            key = pages[slot, 0, :, columns].astype(jnp.float32)
            value = pages[slot, 1, :, columns].astype(jnp.float32)
            k_buf[place, :] = jnp.where(seen, key, spare).astype(jnp.bfloat16)
            v_buf[place, 0:entries] = jnp.where(seen, value, 0.0).astype(jnp.bfloat16)
            v_buf[place, entries:2 * entries] = jnp.where(seen, 1.0, 0.0).astype(jnp.bfloat16)
            return unused

        lax.fori_loop(0, capacity, lay, 0)
        some = table[1, s, 0] > 0
        stat = jnp.zeros((tokens, entries), jnp.float32)
        for block in range(group_heads // 2):
            at = block * 2 * entries
            pair = q_buf[s, h, :, at:at + 2 * entries]
            rows = jnp.concatenate([pair[:, :entries], pair[:, entries:]], axis=0)
            scores = lax.dot_general(
                rows, k_buf[...], (((1,), (1,)), ((), ())), preferred_element_type=jnp.float32
            )
            top, both = softmax_block(scores, v_buf[...])
            weight_sum = both[:, entries:]
            mean = (both[:, :entries] / jnp.maximum(weight_sum, 1.0)).astype(jnp.bfloat16)
            top = jnp.where(some, top, NEG_FILL)
            for k in range(2):
                part[s, h, :, at + k * entries:at + (k + 1) * entries] = mean[k * tokens:(k + 1) * tokens]
                head = 2 * block + k
                stat = jnp.where(lane == head, top[k * tokens:(k + 1) * tokens], stat)
                stat = jnp.where(lane == group_heads + head, weight_sum[k * tokens:(k + 1) * tokens], stat)
        part_stat[s, h] = stat.T[0:2 * group_heads]

    def unit(s, h):
        compute(s, h)

        @pl.when((s > me) & jnp.logical_not(has_left))
        def _():
            for copy in part_copies(s, h, 0):
                copy.start()

        @pl.when((s < me) & jnp.logical_not(has_right))
        def _():
            for copy in part_copies(s, h, 1):
                copy.start()

    def own(h, unused):
        compute(me, h)
        return unused

    lax.fori_loop(0, kv_heads, own, 0)

    def outward(index, unused):
        distance = 1 + index // kv_heads
        h = index % kv_heads
        for s, inside in ((me - distance, me >= distance), (me + distance, me + distance < stores)):
            @pl.when(inside)
            def _():
                q_copy(s, h, 0).wait_recv()
                pass_query(s, h)

        def each(turn, unused):
            s = me + (2 * turn - 1) * distance

            @pl.when((s >= 0) & (s < stores))
            def _():
                unit(s, h)

            return unused

        return lax.fori_loop(0, 2, each, unused)

    lax.fori_loop(0, (stores - 1) * kv_heads, outward, 0)

    def take_in(s, h, side):
        for copy in part_copies(s, h, side):
            copy.wait_recv()
        mine = part_stat[s, h].T
        theirs = inc_stat[side, s, h].T
        stat = jnp.zeros((tokens, entries), jnp.float32)
        for head in range(group_heads):
            columns = slice(head * entries, (head + 1) * entries)

            def state(where, numbers):
                return (
                    where[:, columns].astype(jnp.float32),
                    jnp.broadcast_to(numbers[:, head:head + 1], (tokens, entries)),
                    jnp.broadcast_to(numbers[:, group_heads + head:group_heads + head + 1], (tokens, entries)),
                )

            mean, top, total = merge(state(part.at[s, h], mine), state(inc.at[side, s, h], theirs))
            part[s, h, :, columns] = mean.astype(jnp.bfloat16)
            stat = jnp.where(lane == head, top, stat)
            stat = jnp.where(lane == group_heads + head, total, stat)
        part_stat[s, h] = stat.T[0:2 * group_heads]

    key_index = lax.broadcasted_iota(jnp.int32, (2 * tokens, 2 * tokens), 1)
    query_index = lax.broadcasted_iota(jnp.int32, (2 * tokens, 2 * tokens), 0) % tokens
    allowed = (key_index - tokens <= query_index) & (key_index >= (1 - rep_id) * tokens)

    def fresh(h, unused):
        columns = pl.ds(pl.multiple_of(h * entries, entries), entries)
        key = new_kv[0, :, columns]
        value = jnp.concatenate(
            [new_kv[1, :, columns], jnp.ones((2 * tokens, entries), jnp.bfloat16)], axis=1
        )
        mine = part_stat[me, h].T
        stat = jnp.zeros((tokens, entries), jnp.float32)
        for block in range(group_heads // 2):
            at = block * 2 * entries
            pair = q_buf[me, h, :, at:at + 2 * entries]
            rows = jnp.concatenate([pair[:, :entries], pair[:, entries:]], axis=0)
            scores = lax.dot_general(
                rows, key, (((1,), (1,)), ((), ())), preferred_element_type=jnp.float32
            )
            top, both = softmax_block(jnp.where(allowed, scores, NEG_FILL), value)
            for k in range(2):
                head = 2 * block + k
                columns_k = slice(at + k * entries, at + (k + 1) * entries)
                span = slice(k * tokens, (k + 1) * tokens)
                total = both[span, entries:]
                mean, peak, total = merge(
                    (both[span, :entries] / total, jnp.broadcast_to(top[span], (tokens, entries)), total),
                    (
                        part[me, h, :, columns_k].astype(jnp.float32),
                        jnp.broadcast_to(mine[:, head:head + 1], (tokens, entries)),
                        jnp.broadcast_to(mine[:, group_heads + head:group_heads + head + 1], (tokens, entries)),
                    ),
                )
                part[me, h, :, columns_k] = mean.astype(jnp.bfloat16)
                stat = jnp.where(lane == head, peak, stat)
                stat = jnp.where(lane == group_heads + head, total, stat)
        part_stat[me, h] = stat.T[0:2 * group_heads]
        return unused

    lax.fori_loop(0, kv_heads, fresh, 0)

    def inward(index, unused):
        distance = stores - 1 - index // kv_heads
        h = index % kv_heads

        @pl.when((me + distance < stores) & has_left)
        def _():
            take_in(me + distance, h, 0)
            for copy in part_copies(me + distance, h, 0):
                copy.start()

        @pl.when((me >= distance) & has_right)
        def _():
            take_in(me - distance, h, 1)
            for copy in part_copies(me - distance, h, 1):
                copy.start()

        return unused

    lax.fori_loop(0, (stores - 1) * kv_heads, inward, 0)

    def finish(h, unused):
        @pl.when(has_left)
        def _():
            take_in(me, h, 0)

        @pl.when(has_right)
        def _():
            take_in(me, h, 1)

        width = pl.ds(pl.multiple_of(h * head_width, head_width), head_width)
        out_ref[:, width] = part[me, h]
        return unused

    lax.fori_loop(0, kv_heads, finish, 0)

    def drain(index, unused):
        s = index // kv_heads
        h = index % kv_heads

        @pl.when((s <= me) & has_right)
        def _():
            q_copy(s, h, 0).wait_send()

        @pl.when((s >= me) & has_left)
        def _():
            q_copy(s, h, 1).wait_send()

        @pl.when(s != me)
        def _():
            for copy in part_copies(s, h, 0):
                copy.wait_send()

        return unused

    lax.fori_loop(0, stores * kv_heads, drain, 0)


def buffers_of(stores, kv_heads, group_heads, capacity, tokens, page_len):
    head_width = group_heads * HEAD_ENTRIES
    stat_rows = 2 * group_heads
    return [
        pltpu.VMEM((stores, kv_heads, tokens, head_width), jnp.bfloat16),
        pltpu.VMEM((stores, kv_heads, tokens, head_width), jnp.bfloat16),
        pltpu.VMEM((stores, kv_heads, stat_rows, tokens), jnp.float32),
        pltpu.VMEM((2, stores, kv_heads, tokens, head_width), jnp.bfloat16),
        pltpu.VMEM((2, stores, kv_heads, stat_rows, tokens), jnp.float32),
        pltpu.VMEM((capacity * page_len, HEAD_ENTRIES), jnp.bfloat16),
        pltpu.VMEM((capacity * page_len, 2 * HEAD_ENTRIES), jnp.bfloat16),
        pltpu.SemaphoreType.DMA((2, stores, kv_heads)),
        pltpu.SemaphoreType.DMA((stores, kv_heads)),
        pltpu.SemaphoreType.DMA((stores, kv_heads)),
        pltpu.SemaphoreType.DMA((2, stores, kv_heads)),
        pltpu.SemaphoreType.DMA((stores, kv_heads)),
        pltpu.SemaphoreType.DMA((2, stores, kv_heads)),
    ]


def attend(table, own_queries, page_store, new_kv, stores, kv_heads):
    tokens = own_queries.shape[0]
    page_len = page_store.shape[2]
    group_heads = own_queries.shape[1] // (kv_heads * HEAD_ENTRIES)
    capacity = table.shape[2]
    sizes = (stores, kv_heads, group_heads, capacity, tokens, page_len)
    vmem = pl.BlockSpec(memory_space=pltpu.VMEM)
    pairs = stores * capacity * page_len * tokens * kv_heads * group_heads
    return pl.pallas_call(
        functools.partial(attend_kernel, *sizes),
        out_shape=jax.ShapeDtypeStruct(own_queries.shape, jnp.bfloat16),
        in_specs=[pl.BlockSpec(memory_space=pltpu.SMEM), vmem, vmem, vmem],
        out_specs=vmem,
        scratch_shapes=buffers_of(*sizes),
        compiler_params=pltpu.CompilerParams(
            collective_id=0, has_side_effects=True, vmem_limit_bytes=KERNEL_BYTES
        ),
        cost_estimate=pl.CostEstimate(
            flops=4 * pairs * HEAD_ENTRIES, bytes_accessed=2 * page_store.size, transcendentals=pairs
        ),
        name="attend_pages",
    )(table, own_queries, page_store, new_kv)


def push_shards(
    queries, hidden, key_value_weight, page_store, prefix_holder, prefix_slot, prefix_len, new_owner
):
    store_id = lax.axis_index("store")
    rep_id = lax.axis_index("rep")
    stores = lax.axis_size("store")
    tensors = lax.axis_size("tensor")
    tokens = queries.shape[1]
    page_len = page_store.shape[2]
    local_width = page_store.shape[3]
    kv_heads = local_width // HEAD_ENTRIES
    quarter_rows = hidden.shape[2]
    list_len = prefix_slot.shape[1]
    capacity = 2 * max(2, list_len // (2 * stores))
    table = held_table(
        prefix_holder[:, :, 0], prefix_slot, prefix_len, capacity, page_len, store_id
    )
    weight_full = lax.all_gather(key_value_weight, "rep", axis=0, tiled=True)
    weight_five = weight_full.reshape(quarter_rows, tensors, kv_heads, 2, HEAD_ENTRIES)
    partial_value = jnp.einsum(
        "tc,cghkd->gkthd", hidden[0], weight_five, preferred_element_type=jnp.float32
    )
    summed = lax.psum_scatter(
        partial_value.reshape(tensors * 2 * tokens, local_width).astype(jnp.bfloat16),
        "tensor",
        scatter_dimension=0,
        tiled=True,
    )
    own_kv = summed.reshape(2, tokens, local_width)
    spread = lax.all_gather(own_kv[None], "store", axis=0, tiled=True)
    owner_row = lax.dynamic_index_in_dim(new_owner, rep_id, 0, keepdims=False)
    source = jnp.argmax(owner_row == store_id)
    new_page = lax.dynamic_index_in_dim(spread, source, 0, keepdims=False)
    added_pages = new_page.reshape(1, 1, 2, tokens, local_width)
    earlier = from_behind(own_kv, "rep", 1)
    new_kv = jnp.concatenate([earlier, own_kv], axis=1)
    attended = attend(table, queries[0], page_store, new_kv, stores, kv_heads)
    return (attended[None], added_pages)


def held_in_vmem(mesh, queries, page_store):
    stores = mesh.shape["store"]
    page_bytes = 2 * page_store.size // (mesh.shape["group"] * stores * mesh.shape["tensor"])
    query_bytes = 2 * queries.size // (mesh.shape["group"] * mesh.shape["tensor"] * mesh.shape["rep"])
    return page_bytes + 4 * query_bytes < KERNEL_BYTES // 2


def solution(mesh):
    placed = (
        P(("group", "store"), "rep", "tensor"),
        P(("group", "store"), "rep", "tensor"),
        P(("tensor", "rep"), None),
        P(("group", "store"), None, None, "tensor"),
        P("group", None, None),
        P("group", None),
        P("group"),
        P(None, "group"),
    )
    build = functools.partial(
        jax.shard_map,
        mesh=mesh,
        in_specs=placed,
        out_specs=(
            P(("group", "store"), "rep", "tensor"),
            P(("group", "store"), "rep", None, None, "tensor"),
        ),
        check_vma=False,
    )

    def whole(*arrays):
        fits = held_in_vmem(mesh, arrays[0], arrays[3])
        return build(push_shards if fits else pull_shards)(*arrays)

    return whole
```

```python
import functools
import math

import jax
import jax.numpy as jnp
from jax import lax
from jax.experimental import pallas as pl
from jax.experimental.pallas import tpu as pltpu
from jax.sharding import PartitionSpec as P

HEAD_ENTRIES = 128


NEG_FILL = -1e30


def from_behind(block, axis, distance):
    devices = range(lax.axis_size(axis))
    route = [(i - distance, i) for i in devices if i - distance in devices]
    return lax.ppermute(block, axis, route)


def attend_block(running, query_matrix, key_rows, values, allowed):
    row_max, weight_sum, weighted = running
    score_scale = 1.0 / math.sqrt(key_rows.shape[-1])
    scores = (
        jnp.einsum("rhgd,khd->hgrk", query_matrix, key_rows, preferred_element_type=jnp.float32)
        * score_scale
    )
    scores = jnp.where(allowed, scores, NEG_FILL)
    fresh_max = jnp.maximum(row_max, jnp.max(scores, axis=-1))
    shrink = jnp.exp(row_max - fresh_max)
    weights = jnp.where(allowed, jnp.exp(scores - fresh_max[..., None]), 0.0)
    weight_sum = weight_sum * shrink + jnp.sum(weights, axis=-1)
    weighted = weighted * shrink[..., None] + jnp.einsum(
        "hgrk,khd->hgrd", weights.astype(jnp.bfloat16), values, preferred_element_type=jnp.float32
    )
    return (fresh_max, weight_sum, weighted)


def start_carry(kv_heads, serving_groups, row_count, head_size):
    return (
        jnp.full((kv_heads, serving_groups, row_count), NEG_FILL, jnp.float32),
        jnp.zeros((kv_heads, serving_groups, row_count), jnp.float32),
        jnp.zeros((kv_heads, serving_groups, row_count, head_size), jnp.float32),
    )


def scan_pages(running, query_matrix, pulled, token_ok):
    page_count = pulled.shape[0]
    page_len = pulled.shape[2]
    kv_heads = query_matrix.shape[1]
    head_size = query_matrix.shape[3]
    per_block = math.gcd(page_count, max(1, 1024 // page_len))
    blocks = page_count // per_block
    page_blocks = pulled.reshape(blocks, per_block, 2, page_len, kv_heads, head_size)
    ok_blocks = token_ok.reshape(blocks, per_block * page_len)

    def visit_block(state_now, block_item):
        page_block, block_ok = block_item
        key_rows = page_block[:, 0].reshape(per_block * page_len, kv_heads, head_size)
        values = page_block[:, 1].reshape(per_block * page_len, kv_heads, head_size)
        return (
            attend_block(state_now, query_matrix, key_rows, values, block_ok[None, None, None, :]),
            None,
        )

    running, unused = lax.scan(visit_block, running, (page_blocks, ok_blocks))
    return running


def pull_plan(holders, places):
    member = (holders[:, :, None] == jnp.arange(places, dtype=jnp.int32)[None, None, :]).astype(
        jnp.int32
    )
    ranking = jnp.sum((jnp.cumsum(member, axis=1) - 1) * member, axis=-1)
    return (holders, ranking)


def send_pages(page_store, holders_part, ranking, slots, capacity, store_id):
    chosen = (holders_part == store_id)[:, None, :] & (
        ranking[:, None, :] == jnp.arange(capacity, dtype=jnp.int32)[None, :, None]
    )
    slot_of = jnp.sum(jnp.where(chosen, slots[:, None, :], 0), axis=-1)
    return page_store[slot_of.reshape(-1)]


def receive_order(received, holders_part, ranking, store_id, capacity):
    own_holders = lax.dynamic_index_in_dim(holders_part, store_id, 0, keepdims=False)
    my_rank = lax.dynamic_index_in_dim(ranking, store_id, 0, keepdims=False)
    return received[own_holders * capacity + my_rank]


def pull_shards(
    queries, hidden, key_value_weight, page_store, prefix_holder, prefix_slot, prefix_len, new_owner
):
    store_id = lax.axis_index("store")
    rep_id = lax.axis_index("rep")
    stores = lax.axis_size("store")
    tensors = lax.axis_size("tensor")
    tokens = queries.shape[1]
    page_len = page_store.shape[2]
    local_width = page_store.shape[3]
    kv_heads = local_width // HEAD_ENTRIES
    serving_groups = queries.shape[2] // local_width
    quarter_rows = hidden.shape[2]
    own_rows = hidden[0]
    weight_full = lax.all_gather(key_value_weight, "rep", axis=0, tiled=True)
    weight_five = weight_full.reshape(quarter_rows, tensors, kv_heads, 2, HEAD_ENTRIES)
    partial_value = jnp.einsum(
        "tc,cghkd->gkthd", own_rows, weight_five, preferred_element_type=jnp.float32
    )
    summed = lax.psum_scatter(
        partial_value.reshape(tensors * 2 * tokens, kv_heads * HEAD_ENTRIES).astype(jnp.bfloat16),
        "tensor",
        scatter_dimension=0,
        tiled=True,
    )
    own_kv = summed.reshape(2, tokens, kv_heads * HEAD_ENTRIES)
    spread = lax.all_gather(own_kv[None], "store", axis=0, tiled=True)
    owner_row = lax.dynamic_index_in_dim(new_owner, rep_id, 0, keepdims=False)
    owner_pick = (owner_row == store_id).astype(jnp.bfloat16)
    new_page = jnp.einsum(
        "n,nktc->ktc", owner_pick, spread, preferred_element_type=jnp.float32
    ).astype(jnp.bfloat16)
    added_pages = new_page.reshape(1, 1, 2, tokens, kv_heads * HEAD_ENTRIES)
    earlier = from_behind(own_kv, "rep", 1)
    new_keys = jnp.concatenate([earlier[0], own_kv[0]], 0).reshape(
        2 * tokens, kv_heads, HEAD_ENTRIES
    )
    new_values = jnp.concatenate([earlier[1], own_kv[1]], 0).reshape(
        2 * tokens, kv_heads, HEAD_ENTRIES
    )
    key_index = jnp.arange(2 * tokens, dtype=jnp.int32)[None, :]
    query_index = jnp.arange(tokens, dtype=jnp.int32)[:, None]
    allowed_new = jnp.where(key_index < tokens, rep_id > 0, key_index - tokens <= query_index)
    my_len = lax.dynamic_index_in_dim(prefix_len, store_id, 0, keepdims=False)
    list_len = prefix_slot.shape[1]
    holders = prefix_holder[:, :, 0]
    query_matrix = queries[0].reshape(tokens, kv_heads, serving_groups, HEAD_ENTRIES)
    capacity = 2 * max(2, list_len // (2 * stores))
    holders_part, ranking = pull_plan(holders, stores)
    outgoing = send_pages(page_store, holders_part, ranking, prefix_slot, capacity, store_id)
    incoming = lax.all_to_all(outgoing, "store", split_axis=0, concat_axis=0, tiled=True)
    pulled = receive_order(incoming, holders_part, ranking, store_id, capacity)
    token_ok = jnp.arange(list_len * page_len, dtype=jnp.int32) < my_len
    running = scan_pages(
        start_carry(kv_heads, serving_groups, tokens, HEAD_ENTRIES), query_matrix, pulled, token_ok
    )
    running = attend_block(running, query_matrix, new_keys, new_values, allowed_new[None, None])
    row_max, weight_sum, weighted = running
    result = (
        (weighted / weight_sum[..., None])
        .transpose(2, 0, 1, 3)
        .reshape(1, tokens, kv_heads * serving_groups * HEAD_ENTRIES)
    )
    return (result.astype(jnp.bfloat16), added_pages)


MESH = pl.DeviceIdType.MESH
SCORE_FACTOR = math.log2(math.e) / math.sqrt(HEAD_ENTRIES)
KERNEL_BYTES = 60 * 2**20


def held_table(holders, slots, lengths, capacity, page_len, store_id):
    count = holders.shape[1]
    place = jnp.arange(count, dtype=jnp.int32)
    same = (holders[:, :, None] == holders[:, None, :]) & (place[None, None, :] < place[None, :, None])
    ranking = jnp.sum(same.astype(jnp.int32), axis=-1)
    chosen = (holders == store_id)[:, None, :] & (
        ranking[:, None, :] == jnp.arange(capacity, dtype=jnp.int32)[None, :, None]
    )
    visible = jnp.clip(lengths[:, None] - place[None, :] * page_len, 0, page_len)
    slot_of = jnp.sum(jnp.where(chosen, slots[:, None, :], 0), axis=-1)
    visible_of = jnp.sum(jnp.where(chosen, visible[:, None, :], 0), axis=-1)
    return jnp.stack([slot_of, visible_of])


def merge(first, second):
    out1, max1, sum1 = first
    out2, max2, sum2 = second
    top = jnp.maximum(max1, max2)
    share1 = sum1 * jnp.exp2((max1 - top) * SCORE_FACTOR)
    share2 = sum2 * jnp.exp2((max2 - top) * SCORE_FACTOR)
    total = share1 + share2
    inverse = 1.0 / jnp.maximum(total, 1.0)
    return (out1 * (share1 * inverse) + out2 * (share2 * inverse), top, total)


def attend_kernel(
    stores, tensors, kv_heads, group_heads, capacity, tokens, page_len,
    table, source, q_ref, hidden, weight_hbm, pages_hbm, out_ref, added_ref,
    q_buf, part, part_stat, inc, inc_stat, k_buf, v_buf,
    weight, pages, rows_in, products, terms, kv_buf, other_kv,
    q_send, q_recv, p_send, p_recv, t_send, t_recv,
    load, rows_send, rows_recv, term_send, term_recv, kv_send, kv_recv, other_send, other_recv,
):
    weight_load = pltpu.make_async_copy(weight_hbm, weight, load.at[0])
    page_load = pltpu.make_async_copy(pages_hbm, pages, load.at[1])
    page_load.start()
    weight_load.start()
    me = lax.axis_index("store")
    rep_id = lax.axis_index("rep")
    tensor_id = lax.axis_index("tensor")
    other_rep = 1 - rep_id
    has_left = me > 0
    has_right = me < stores - 1
    entries = HEAD_ENTRIES
    head_width = group_heads * entries

    def q_copy(s, h, side):
        step = 1 if side == 0 else -1
        return pltpu.make_async_remote_copy(
            src_ref=q_buf.at[s, h], dst_ref=q_buf.at[s, h],
            send_sem=q_send.at[side, s, h], recv_sem=q_recv.at[s, h],
            device_id={"store": me + step}, device_id_type=MESH,
        )

    def part_copies(s, h, side):
        step = 1 if side == 0 else -1
        return [
            pltpu.make_async_remote_copy(
                src_ref=source.at[s, h], dst_ref=target.at[side, s, h],
                send_sem=send.at[s, h], recv_sem=recv.at[side, s, h],
                device_id={"store": me + step}, device_id_type=MESH,
            )
            for source, target, send, recv in (
                (part, inc, p_send, p_recv), (part_stat, inc_stat, t_send, t_recv)
            )
        ]

    depth = hidden.shape[1] // 2

    def rows_copy():
        return pltpu.make_async_remote_copy(
            src_ref=hidden.at[:, pl.ds(pl.multiple_of(other_rep * depth, HEAD_ENTRIES), depth)],
            dst_ref=rows_in.at[rep_id],
            send_sem=rows_send, recv_sem=rows_recv,
            device_id={"rep": other_rep}, device_id_type=MESH,
        )

    peers = [(dt, dr) for dt in range(tensors) for dr in range(2) if dt or dr]

    def peer(dt, dr):
        return lax.rem(tensor_id + dt, tensors), lax.rem(rep_id + dr, 2)

    def term_copy(k):
        tensor_to, rep_to = peer(*peers[k])
        return pltpu.make_async_remote_copy(
            src_ref=products.at[tensor_to, rep_to], dst_ref=terms.at[k],
            send_sem=term_send.at[k], recv_sem=term_recv.at[k],
            device_id={"tensor": tensor_to, "rep": rep_to}, device_id_type=MESH,
        )

    def kv_copy(s, side):
        step = 1 if side == 0 else -1
        return pltpu.make_async_remote_copy(
            src_ref=kv_buf.at[s], dst_ref=kv_buf.at[s],
            send_sem=kv_send.at[side, s], recv_sem=kv_recv.at[s],
            device_id={"store": me + step}, device_id_type=MESH,
        )

    def other_copy():
        return pltpu.make_async_remote_copy(
            src_ref=kv_buf.at[me], dst_ref=other_kv,
            send_sem=other_send, recv_sem=other_recv,
            device_id={"rep": other_rep}, device_id_type=MESH,
        )

    barrier = pltpu.get_barrier_semaphore()
    for dt, dr in peers:
        tensor_to, rep_to = peer(dt, dr)
        pl.semaphore_signal(
            barrier, inc=1, device_id={"tensor": tensor_to, "rep": rep_to}, device_id_type=MESH
        )

    @pl.when(has_left)
    def _():
        pl.semaphore_signal(barrier, inc=1, device_id={"store": me - 1}, device_id_type=MESH)

    @pl.when(has_right)
    def _():
        pl.semaphore_signal(barrier, inc=1, device_id={"store": me + 1}, device_id_type=MESH)

    for h in range(kv_heads):
        q_buf[me, h] = q_ref[:, h * head_width:(h + 1) * head_width]

    pl.semaphore_wait(barrier, has_left.astype(jnp.int32) + has_right.astype(jnp.int32) + len(peers))
    rows_copy().start()

    def pass_query(s, h):
        @pl.when((s <= me) & has_right)
        def _():
            q_copy(s, h, 0).start()

        @pl.when((s >= me) & has_left)
        def _():
            q_copy(s, h, 1).start()

    for h in range(kv_heads):
        pass_query(me, h)

    lane = lax.broadcasted_iota(jnp.int32, (tokens, entries), 1)

    def softmax_block(scores, values):
        top = jnp.max(scores, axis=1, keepdims=True)
        weights = jnp.exp2((scores - top) * SCORE_FACTOR).astype(jnp.bfloat16)
        return top, jnp.dot(weights, values, preferred_element_type=jnp.float32)

    def compute(s, h):
        columns = pl.ds(pl.multiple_of(h * entries, entries), entries)
        spare = pages[table[0, s, 0], 0, 0:8, columns].astype(jnp.float32)[0:1]
        row = lax.broadcasted_iota(jnp.int32, (page_len, entries), 0)

        def lay(r, unused):
            slot = table[0, s, r]
            seen = row < table[1, s, r]
            place = pl.ds(pl.multiple_of(r * page_len, page_len), page_len)
            key = pages[slot, 0, :, columns].astype(jnp.float32)
            value = pages[slot, 1, :, columns].astype(jnp.float32)
            k_buf[place, :] = jnp.where(seen, key, spare).astype(jnp.bfloat16)
            v_buf[place, 0:entries] = jnp.where(seen, value, 0.0).astype(jnp.bfloat16)
            v_buf[place, entries:2 * entries] = jnp.where(seen, 1.0, 0.0).astype(jnp.bfloat16)
            return unused

        lax.fori_loop(0, capacity, lay, 0)
        some = table[1, s, 0] > 0
        stat = jnp.zeros((tokens, entries), jnp.float32)
        for block in range(group_heads // 2):
            at = block * 2 * entries
            pair = q_buf[s, h, :, at:at + 2 * entries]
            rows = jnp.concatenate([pair[:, :entries], pair[:, entries:]], axis=0)
            scores = lax.dot_general(
                rows, k_buf[...], (((1,), (1,)), ((), ())), preferred_element_type=jnp.float32
            )
            top, both = softmax_block(scores, v_buf[...])
            weight_sum = both[:, entries:]
            mean = (both[:, :entries] / jnp.maximum(weight_sum, 1.0)).astype(jnp.bfloat16)
            top = jnp.where(some, top, NEG_FILL)
            for k in range(2):
                part[s, h, :, at + k * entries:at + (k + 1) * entries] = mean[k * tokens:(k + 1) * tokens]
                head = 2 * block + k
                stat = jnp.where(lane == head, top[k * tokens:(k + 1) * tokens], stat)
                stat = jnp.where(lane == group_heads + head, weight_sum[k * tokens:(k + 1) * tokens], stat)
        part_stat[s, h] = stat.T[0:2 * group_heads]

    def unit(s, h):
        compute(s, h)

        @pl.when((s > me) & jnp.logical_not(has_left))
        def _():
            for copy in part_copies(s, h, 0):
                copy.start()

        @pl.when((s < me) & jnp.logical_not(has_right))
        def _():
            for copy in part_copies(s, h, 1):
                copy.start()

    def own(h, unused):
        compute(me, h)
        return unused

    page_load.wait()
    lax.fori_loop(0, 1, own, 0)

    rows_in[rep_id] = hidden[:, pl.ds(pl.multiple_of(rep_id * depth, entries), depth)]
    rows_copy().wait_recv()
    weight_load.wait()
    all_rows = rows_in[...].reshape(2 * tokens, depth)
    block_width = 2 * kv_heads * entries
    for t in range(tensors):
        product = jnp.dot(
            all_rows, weight[:, t * block_width:(t + 1) * block_width],
            preferred_element_type=jnp.float32,
        ).astype(jnp.bfloat16)
        for r in range(2):
            products[t, r] = product[r * tokens:(r + 1) * tokens]
    for k in range(len(peers)):
        term_copy(k).start()

    lax.fori_loop(1, kv_heads, own, 0)

    total_kv = products[tensor_id, rep_id].astype(jnp.float32)
    for k in range(len(peers)):
        term_copy(k).wait_recv()
        total_kv = total_kv + terms[k].astype(jnp.float32)
    total_kv = total_kv.astype(jnp.bfloat16)
    for head in range(kv_heads):
        for kind in range(2):
            at = (2 * head + kind) * entries
            kv_buf[me, kind, :, head * entries:(head + 1) * entries] = total_kv[:, at:at + entries]

    def pass_kv(s):
        @pl.when((s <= me) & has_right)
        def _():
            kv_copy(s, 0).start()

        @pl.when((s >= me) & has_left)
        def _():
            kv_copy(s, 1).start()

    other_copy().start()
    pass_kv(me)

    def relay_kv(distance):
        for s, inside in ((me - distance, me >= distance), (me + distance, me + distance < stores)):
            @pl.when(inside)
            def _():
                kv_copy(s, 0).wait_recv()
                pass_kv(s)

    def outward(index, unused):
        distance = 1 + index // kv_heads
        h = index % kv_heads
        for s, inside in ((me - distance, me >= distance), (me + distance, me + distance < stores)):
            @pl.when(inside)
            def _():
                q_copy(s, h, 0).wait_recv()
                pass_query(s, h)

        def each(turn, unused):
            s = me + (2 * turn - 1) * distance

            @pl.when((s >= 0) & (s < stores))
            def _():
                unit(s, h)

            return unused

        unused = lax.fori_loop(0, 2, each, unused)

        @pl.when((h == kv_heads - 1) & (distance > 1))
        def _():
            relay_kv(distance - 1)

        return unused

    lax.fori_loop(0, (stores - 1) * kv_heads, outward, 0)
    other_copy().wait_recv()

    def take_in(s, h, side):
        for copy in part_copies(s, h, side):
            copy.wait_recv()
        mine = part_stat[s, h].T
        theirs = inc_stat[side, s, h].T
        stat = jnp.zeros((tokens, entries), jnp.float32)
        for head in range(group_heads):
            columns = slice(head * entries, (head + 1) * entries)

            def state(where, numbers):
                return (
                    where[:, columns].astype(jnp.float32),
                    jnp.broadcast_to(numbers[:, head:head + 1], (tokens, entries)),
                    jnp.broadcast_to(numbers[:, group_heads + head:group_heads + head + 1], (tokens, entries)),
                )

            mean, top, total = merge(state(part.at[s, h], mine), state(inc.at[side, s, h], theirs))
            part[s, h, :, columns] = mean.astype(jnp.bfloat16)
            stat = jnp.where(lane == head, top, stat)
            stat = jnp.where(lane == group_heads + head, total, stat)
        part_stat[s, h] = stat.T[0:2 * group_heads]

    key_index = lax.broadcasted_iota(jnp.int32, (2 * tokens, 2 * tokens), 1)
    query_index = lax.broadcasted_iota(jnp.int32, (2 * tokens, 2 * tokens), 0) % tokens
    allowed = (key_index - tokens <= query_index) & (key_index >= (1 - rep_id) * tokens)

    def fresh(h, unused):
        columns = pl.ds(pl.multiple_of(h * entries, entries), entries)
        key = jnp.concatenate([other_kv[0, :, columns], kv_buf[me, 0, :, columns]], axis=0)
        value = jnp.concatenate([other_kv[1, :, columns], kv_buf[me, 1, :, columns]], axis=0)
        value = jnp.concatenate([value, jnp.ones((2 * tokens, entries), jnp.bfloat16)], axis=1)
        mine = part_stat[me, h].T
        stat = jnp.zeros((tokens, entries), jnp.float32)
        for block in range(group_heads // 2):
            at = block * 2 * entries
            pair = q_buf[me, h, :, at:at + 2 * entries]
            rows = jnp.concatenate([pair[:, :entries], pair[:, entries:]], axis=0)
            scores = lax.dot_general(
                rows, key, (((1,), (1,)), ((), ())), preferred_element_type=jnp.float32
            )
            top, both = softmax_block(jnp.where(allowed, scores, NEG_FILL), value)
            for k in range(2):
                head = 2 * block + k
                columns_k = slice(at + k * entries, at + (k + 1) * entries)
                span = slice(k * tokens, (k + 1) * tokens)
                total = both[span, entries:]
                mean, peak, total = merge(
                    (both[span, :entries] / total, jnp.broadcast_to(top[span], (tokens, entries)), total),
                    (
                        part[me, h, :, columns_k].astype(jnp.float32),
                        jnp.broadcast_to(mine[:, head:head + 1], (tokens, entries)),
                        jnp.broadcast_to(mine[:, group_heads + head:group_heads + head + 1], (tokens, entries)),
                    ),
                )
                part[me, h, :, columns_k] = mean.astype(jnp.bfloat16)
                stat = jnp.where(lane == head, peak, stat)
                stat = jnp.where(lane == group_heads + head, total, stat)
        part_stat[me, h] = stat.T[0:2 * group_heads]
        return unused

    lax.fori_loop(0, kv_heads, fresh, 0)

    def inward(index, unused):
        distance = stores - 1 - index // kv_heads
        h = index % kv_heads

        @pl.when((me + distance < stores) & has_left)
        def _():
            take_in(me + distance, h, 0)
            for copy in part_copies(me + distance, h, 0):
                copy.start()

        @pl.when((me >= distance) & has_right)
        def _():
            take_in(me - distance, h, 1)
            for copy in part_copies(me - distance, h, 1):
                copy.start()

        return unused

    lax.fori_loop(0, (stores - 1) * kv_heads, inward, 0)

    def finish(h, unused):
        @pl.when(has_left)
        def _():
            take_in(me, h, 0)

        @pl.when(has_right)
        def _():
            take_in(me, h, 1)

        width = pl.ds(pl.multiple_of(h * head_width, head_width), head_width)
        out_ref[:, width] = part[me, h]
        return unused

    relay_kv(stores - 1)
    added_ref[...] = kv_buf[source[0]]
    lax.fori_loop(0, kv_heads, finish, 0)
    rows_copy().wait_send()
    for k in range(len(peers)):
        term_copy(k).wait_send()
    other_copy().wait_send()

    def drain_kv(s, unused):
        @pl.when((s <= me) & has_right)
        def _():
            kv_copy(s, 0).wait_send()

        @pl.when((s >= me) & has_left)
        def _():
            kv_copy(s, 1).wait_send()

        return unused

    lax.fori_loop(0, stores, drain_kv, 0)

    def drain(index, unused):
        s = index // kv_heads
        h = index % kv_heads

        @pl.when((s <= me) & has_right)
        def _():
            q_copy(s, h, 0).wait_send()

        @pl.when((s >= me) & has_left)
        def _():
            q_copy(s, h, 1).wait_send()

        @pl.when(s != me)
        def _():
            for copy in part_copies(s, h, 0):
                copy.wait_send()

        return unused

    lax.fori_loop(0, stores * kv_heads, drain, 0)


def buffers_of(stores, tensors, kv_heads, group_heads, capacity, tokens, page_len, weight, page_store):
    head_width = group_heads * HEAD_ENTRIES
    stat_rows = 2 * group_heads
    block_width = 2 * kv_heads * HEAD_ENTRIES
    return [
        pltpu.VMEM((stores, kv_heads, tokens, head_width), jnp.bfloat16),
        pltpu.VMEM((stores, kv_heads, tokens, head_width), jnp.bfloat16),
        pltpu.VMEM((stores, kv_heads, stat_rows, tokens), jnp.float32),
        pltpu.VMEM((2, stores, kv_heads, tokens, head_width), jnp.bfloat16),
        pltpu.VMEM((2, stores, kv_heads, stat_rows, tokens), jnp.float32),
        pltpu.VMEM((capacity * page_len, HEAD_ENTRIES), jnp.bfloat16),
        pltpu.VMEM((capacity * page_len, 2 * HEAD_ENTRIES), jnp.bfloat16),
        pltpu.VMEM(weight.shape, weight.dtype),
        pltpu.VMEM(page_store.shape, page_store.dtype),
        pltpu.VMEM((2, tokens, weight.shape[0]), jnp.bfloat16),
        pltpu.VMEM((tensors, 2, tokens, block_width), jnp.bfloat16),
        pltpu.VMEM((2 * tensors - 1, tokens, block_width), jnp.bfloat16),
        pltpu.VMEM((stores, 2, tokens, block_width // 2), jnp.bfloat16),
        pltpu.VMEM((2, tokens, block_width // 2), jnp.bfloat16),
        pltpu.SemaphoreType.DMA((2, stores, kv_heads)),
        pltpu.SemaphoreType.DMA((stores, kv_heads)),
        pltpu.SemaphoreType.DMA((stores, kv_heads)),
        pltpu.SemaphoreType.DMA((2, stores, kv_heads)),
        pltpu.SemaphoreType.DMA((stores, kv_heads)),
        pltpu.SemaphoreType.DMA((2, stores, kv_heads)),
        pltpu.SemaphoreType.DMA((2,)),
        pltpu.SemaphoreType.DMA,
        pltpu.SemaphoreType.DMA,
        pltpu.SemaphoreType.DMA((2 * tensors - 1,)),
        pltpu.SemaphoreType.DMA((2 * tensors - 1,)),
        pltpu.SemaphoreType.DMA((2, stores)),
        pltpu.SemaphoreType.DMA((stores,)),
        pltpu.SemaphoreType.DMA,
        pltpu.SemaphoreType.DMA,
    ]


def attend(table, source, own_queries, own_rows, weight, page_store, stores, tensors, kv_heads):
    tokens = own_queries.shape[0]
    page_len = page_store.shape[2]
    group_heads = own_queries.shape[1] // (kv_heads * HEAD_ENTRIES)
    capacity = table.shape[2]
    sizes = (stores, tensors, kv_heads, group_heads, capacity, tokens, page_len)
    smem = pl.BlockSpec(memory_space=pltpu.SMEM)
    vmem = pl.BlockSpec(memory_space=pltpu.VMEM)
    where_it_is = pl.BlockSpec(memory_space=pl.ANY)
    pairs = stores * capacity * page_len * tokens * kv_heads * group_heads
    return pl.pallas_call(
        functools.partial(attend_kernel, *sizes),
        out_shape=(
            jax.ShapeDtypeStruct(own_queries.shape, jnp.bfloat16),
            jax.ShapeDtypeStruct((2, tokens, kv_heads * HEAD_ENTRIES), jnp.bfloat16),
        ),
        in_specs=[smem, smem, vmem, vmem, where_it_is, where_it_is],
        out_specs=(vmem, vmem),
        scratch_shapes=buffers_of(*sizes, weight, page_store),
        compiler_params=pltpu.CompilerParams(
            collective_id=0, has_side_effects=True, vmem_limit_bytes=KERNEL_BYTES
        ),
        cost_estimate=pl.CostEstimate(
            flops=4 * pairs * HEAD_ENTRIES, bytes_accessed=2 * page_store.size, transcendentals=pairs
        ),
        name="attend_pages",
    )(table, source, own_queries, own_rows, weight, page_store)


def push_shards(
    queries, hidden, key_value_weight, page_store, prefix_holder, prefix_slot, prefix_len, new_owner
):
    store_id = lax.axis_index("store")
    rep_id = lax.axis_index("rep")
    stores = lax.axis_size("store")
    tensors = lax.axis_size("tensor")
    page_len = page_store.shape[2]
    kv_heads = page_store.shape[3] // HEAD_ENTRIES
    list_len = prefix_slot.shape[1]
    capacity = 2 * max(2, list_len // (2 * stores))
    table = held_table(
        prefix_holder[:, :, 0], prefix_slot, prefix_len, capacity, page_len, store_id
    )
    owner_row = lax.dynamic_index_in_dim(new_owner, rep_id, 0, keepdims=False)
    request = jnp.arange(stores, dtype=jnp.int32)
    source = jnp.sum(jnp.where(owner_row == store_id, request, 0), keepdims=True)
    attended, added = attend(
        table, source, queries[0], hidden[0], key_value_weight, page_store, stores, tensors, kv_heads
    )
    return (attended[None], added[None, None])


def held_in_vmem(mesh, queries, page_store):
    stores = mesh.shape["store"]
    page_bytes = 2 * page_store.size // (mesh.shape["group"] * stores * mesh.shape["tensor"])
    query_bytes = 2 * queries.size // (mesh.shape["group"] * mesh.shape["tensor"] * mesh.shape["rep"])
    return page_bytes + 4 * query_bytes < KERNEL_BYTES // 2


def solution(mesh):
    placed = (
        P(("group", "store"), "rep", "tensor"),
        P(("group", "store"), "rep", "tensor"),
        P(("tensor", "rep"), None),
        P(("group", "store"), None, None, "tensor"),
        P("group", None, None),
        P("group", None),
        P("group"),
        P(None, "group"),
    )
    build = functools.partial(
        jax.shard_map,
        mesh=mesh,
        in_specs=placed,
        out_specs=(
            P(("group", "store"), "rep", "tensor"),
            P(("group", "store"), "rep", None, None, "tensor"),
        ),
        check_vma=False,
    )

    def whole(*arrays):
        fits = held_in_vmem(mesh, arrays[0], arrays[3])
        return build(push_shards if fits else pull_shards)(*arrays)

    return whole
```

```python
import functools
import math

import jax
import jax.numpy as jnp
from jax import lax
from jax.experimental import pallas as pl
from jax.experimental.pallas import tpu as pltpu
from jax.sharding import PartitionSpec as P

HEAD_ENTRIES = 128


NEG_FILL = -1e30


def from_behind(block, axis, distance):
    devices = range(lax.axis_size(axis))
    route = [(i - distance, i) for i in devices if i - distance in devices]
    return lax.ppermute(block, axis, route)


def attend_block(running, query_matrix, key_rows, values, allowed):
    row_max, weight_sum, weighted = running
    score_scale = 1.0 / math.sqrt(key_rows.shape[-1])
    scores = (
        jnp.einsum("rhgd,khd->hgrk", query_matrix, key_rows, preferred_element_type=jnp.float32)
        * score_scale
    )
    scores = jnp.where(allowed, scores, NEG_FILL)
    fresh_max = jnp.maximum(row_max, jnp.max(scores, axis=-1))
    shrink = jnp.exp(row_max - fresh_max)
    weights = jnp.where(allowed, jnp.exp(scores - fresh_max[..., None]), 0.0)
    weight_sum = weight_sum * shrink + jnp.sum(weights, axis=-1)
    weighted = weighted * shrink[..., None] + jnp.einsum(
        "hgrk,khd->hgrd", weights.astype(jnp.bfloat16), values, preferred_element_type=jnp.float32
    )
    return (fresh_max, weight_sum, weighted)


def start_carry(kv_heads, serving_groups, row_count, head_size):
    return (
        jnp.full((kv_heads, serving_groups, row_count), NEG_FILL, jnp.float32),
        jnp.zeros((kv_heads, serving_groups, row_count), jnp.float32),
        jnp.zeros((kv_heads, serving_groups, row_count, head_size), jnp.float32),
    )


def scan_pages(running, query_matrix, pulled, token_ok):
    page_count = pulled.shape[0]
    page_len = pulled.shape[2]
    kv_heads = query_matrix.shape[1]
    head_size = query_matrix.shape[3]
    per_block = math.gcd(page_count, max(1, 1024 // page_len))
    blocks = page_count // per_block
    page_blocks = pulled.reshape(blocks, per_block, 2, page_len, kv_heads, head_size)
    ok_blocks = token_ok.reshape(blocks, per_block * page_len)

    def visit_block(state_now, block_item):
        page_block, block_ok = block_item
        key_rows = page_block[:, 0].reshape(per_block * page_len, kv_heads, head_size)
        values = page_block[:, 1].reshape(per_block * page_len, kv_heads, head_size)
        return (
            attend_block(state_now, query_matrix, key_rows, values, block_ok[None, None, None, :]),
            None,
        )

    running, unused = lax.scan(visit_block, running, (page_blocks, ok_blocks))
    return running


def pull_plan(holders, places):
    member = (holders[:, :, None] == jnp.arange(places, dtype=jnp.int32)[None, None, :]).astype(
        jnp.int32
    )
    ranking = jnp.sum((jnp.cumsum(member, axis=1) - 1) * member, axis=-1)
    return (holders, ranking)


def send_pages(page_store, holders_part, ranking, slots, capacity, store_id):
    chosen = (holders_part == store_id)[:, None, :] & (
        ranking[:, None, :] == jnp.arange(capacity, dtype=jnp.int32)[None, :, None]
    )
    slot_of = jnp.sum(jnp.where(chosen, slots[:, None, :], 0), axis=-1)
    return page_store[slot_of.reshape(-1)]


def receive_order(received, holders_part, ranking, store_id, capacity):
    own_holders = lax.dynamic_index_in_dim(holders_part, store_id, 0, keepdims=False)
    my_rank = lax.dynamic_index_in_dim(ranking, store_id, 0, keepdims=False)
    return received[own_holders * capacity + my_rank]


def pull_shards(
    queries, hidden, key_value_weight, page_store, prefix_holder, prefix_slot, prefix_len, new_owner
):
    store_id = lax.axis_index("store")
    rep_id = lax.axis_index("rep")
    stores = lax.axis_size("store")
    tensors = lax.axis_size("tensor")
    tokens = queries.shape[1]
    page_len = page_store.shape[2]
    local_width = page_store.shape[3]
    kv_heads = local_width // HEAD_ENTRIES
    serving_groups = queries.shape[2] // local_width
    quarter_rows = hidden.shape[2]
    own_rows = hidden[0]
    weight_full = lax.all_gather(key_value_weight, "rep", axis=0, tiled=True)
    weight_five = weight_full.reshape(quarter_rows, tensors, kv_heads, 2, HEAD_ENTRIES)
    partial_value = jnp.einsum(
        "tc,cghkd->gkthd", own_rows, weight_five, preferred_element_type=jnp.float32
    )
    summed = lax.psum_scatter(
        partial_value.reshape(tensors * 2 * tokens, kv_heads * HEAD_ENTRIES).astype(jnp.bfloat16),
        "tensor",
        scatter_dimension=0,
        tiled=True,
    )
    own_kv = summed.reshape(2, tokens, kv_heads * HEAD_ENTRIES)
    spread = lax.all_gather(own_kv[None], "store", axis=0, tiled=True)
    owner_row = lax.dynamic_index_in_dim(new_owner, rep_id, 0, keepdims=False)
    owner_pick = (owner_row == store_id).astype(jnp.bfloat16)
    new_page = jnp.einsum(
        "n,nktc->ktc", owner_pick, spread, preferred_element_type=jnp.float32
    ).astype(jnp.bfloat16)
    added_pages = new_page.reshape(1, 1, 2, tokens, kv_heads * HEAD_ENTRIES)
    earlier = from_behind(own_kv, "rep", 1)
    new_keys = jnp.concatenate([earlier[0], own_kv[0]], 0).reshape(
        2 * tokens, kv_heads, HEAD_ENTRIES
    )
    new_values = jnp.concatenate([earlier[1], own_kv[1]], 0).reshape(
        2 * tokens, kv_heads, HEAD_ENTRIES
    )
    key_index = jnp.arange(2 * tokens, dtype=jnp.int32)[None, :]
    query_index = jnp.arange(tokens, dtype=jnp.int32)[:, None]
    allowed_new = jnp.where(key_index < tokens, rep_id > 0, key_index - tokens <= query_index)
    my_len = lax.dynamic_index_in_dim(prefix_len, store_id, 0, keepdims=False)
    list_len = prefix_slot.shape[1]
    holders = prefix_holder[:, :, 0]
    query_matrix = queries[0].reshape(tokens, kv_heads, serving_groups, HEAD_ENTRIES)
    capacity = 2 * max(2, list_len // (2 * stores))
    holders_part, ranking = pull_plan(holders, stores)
    outgoing = send_pages(page_store, holders_part, ranking, prefix_slot, capacity, store_id)
    incoming = lax.all_to_all(outgoing, "store", split_axis=0, concat_axis=0, tiled=True)
    pulled = receive_order(incoming, holders_part, ranking, store_id, capacity)
    token_ok = jnp.arange(list_len * page_len, dtype=jnp.int32) < my_len
    running = scan_pages(
        start_carry(kv_heads, serving_groups, tokens, HEAD_ENTRIES), query_matrix, pulled, token_ok
    )
    running = attend_block(running, query_matrix, new_keys, new_values, allowed_new[None, None])
    row_max, weight_sum, weighted = running
    result = (
        (weighted / weight_sum[..., None])
        .transpose(2, 0, 1, 3)
        .reshape(1, tokens, kv_heads * serving_groups * HEAD_ENTRIES)
    )
    return (result.astype(jnp.bfloat16), added_pages)


MESH = pl.DeviceIdType.MESH
SCORE_FACTOR = math.log2(math.e) / math.sqrt(HEAD_ENTRIES)
KERNEL_BYTES = 60 * 2**20


def held_table(holders, slots, capacity, store_id):
    count = holders.shape[1]
    place = jnp.arange(count, dtype=jnp.int32)
    same = (holders[:, :, None] == holders[:, None, :]) & (place[None, None, :] < place[None, :, None])
    ranking = jnp.sum(same.astype(jnp.int32), axis=-1)
    chosen = (holders == store_id)[:, None, :] & (
        ranking[:, None, :] == jnp.arange(capacity, dtype=jnp.int32)[None, :, None]
    )
    entry = slots * count + place[None, :] + 1
    return jnp.sum(jnp.where(chosen, entry[:, None, :], 0), axis=-1)


def merge(first, second):
    out1, max1, sum1 = first
    out2, max2, sum2 = second
    top = jnp.maximum(max1, max2)
    share1 = sum1 * jnp.exp2((max1 - top) * SCORE_FACTOR)
    share2 = sum2 * jnp.exp2((max2 - top) * SCORE_FACTOR)
    total = share1 + share2
    inverse = 1.0 / jnp.maximum(total, 1.0)
    return (out1 * (share1 * inverse) + out2 * (share2 * inverse), top, total)


def attend_kernel(
    list_len, stores, tensors, kv_heads, group_heads, capacity, tokens, page_len,
    table, lengths, new_owner, q_ref, hidden, weight_hbm, pages_hbm, out_ref, added_ref,
    q_buf, part, part_stat, inc, inc_stat, k_buf, v_buf,
    weight, pages, rows_in, products, terms, kv_buf, other_kv,
    q_send, q_recv, p_send, p_recv, t_send, t_recv,
    load, rows_send, rows_recv, term_send, term_recv, kv_send, kv_recv, other_send, other_recv,
):
    weight_load = pltpu.make_async_copy(weight_hbm, weight, load.at[0])
    page_load = pltpu.make_async_copy(pages_hbm, pages, load.at[1])
    page_load.start()
    weight_load.start()
    me = lax.axis_index("store")
    rep_id = lax.axis_index("rep")
    tensor_id = lax.axis_index("tensor")
    other_rep = 1 - rep_id
    has_left = me > 0
    has_right = me < stores - 1
    entries = HEAD_ENTRIES
    head_width = group_heads * entries

    def q_copy(s, h, side):
        step = 1 if side == 0 else -1
        return pltpu.make_async_remote_copy(
            src_ref=q_buf.at[s, h], dst_ref=q_buf.at[s, h],
            send_sem=q_send.at[side, s, h], recv_sem=q_recv.at[s, h],
            device_id={"store": me + step}, device_id_type=MESH,
        )

    def part_copies(s, h, side):
        step = 1 if side == 0 else -1
        return [
            pltpu.make_async_remote_copy(
                src_ref=source.at[s, h], dst_ref=target.at[side, s, h],
                send_sem=send.at[s, h], recv_sem=recv.at[side, s, h],
                device_id={"store": me + step}, device_id_type=MESH,
            )
            for source, target, send, recv in (
                (part, inc, p_send, p_recv), (part_stat, inc_stat, t_send, t_recv)
            )
        ]

    depth = hidden.shape[1] // 2

    def rows_copy():
        return pltpu.make_async_remote_copy(
            src_ref=hidden.at[:, pl.ds(pl.multiple_of(other_rep * depth, HEAD_ENTRIES), depth)],
            dst_ref=rows_in.at[rep_id],
            send_sem=rows_send, recv_sem=rows_recv,
            device_id={"rep": other_rep}, device_id_type=MESH,
        )

    peers = [(dt, dr) for dt in range(tensors) for dr in range(2) if dt or dr]

    def peer(dt, dr):
        return lax.rem(tensor_id + dt, tensors), lax.rem(rep_id + dr, 2)

    def term_copy(k):
        tensor_to, rep_to = peer(*peers[k])
        return pltpu.make_async_remote_copy(
            src_ref=products.at[tensor_to, rep_to], dst_ref=terms.at[k],
            send_sem=term_send.at[k], recv_sem=term_recv.at[k],
            device_id={"tensor": tensor_to, "rep": rep_to}, device_id_type=MESH,
        )

    def kv_copy(s, side):
        step = 1 if side == 0 else -1
        return pltpu.make_async_remote_copy(
            src_ref=kv_buf.at[s], dst_ref=kv_buf.at[s],
            send_sem=kv_send.at[side, s], recv_sem=kv_recv.at[s],
            device_id={"store": me + step}, device_id_type=MESH,
        )

    def other_copy():
        return pltpu.make_async_remote_copy(
            src_ref=kv_buf.at[me], dst_ref=other_kv,
            send_sem=other_send, recv_sem=other_recv,
            device_id={"rep": other_rep}, device_id_type=MESH,
        )

    barrier = pltpu.get_barrier_semaphore()
    for dt, dr in peers:
        tensor_to, rep_to = peer(dt, dr)
        pl.semaphore_signal(
            barrier, inc=1, device_id={"tensor": tensor_to, "rep": rep_to}, device_id_type=MESH
        )

    @pl.when(has_left)
    def _():
        pl.semaphore_signal(barrier, inc=1, device_id={"store": me - 1}, device_id_type=MESH)

    @pl.when(has_right)
    def _():
        pl.semaphore_signal(barrier, inc=1, device_id={"store": me + 1}, device_id_type=MESH)

    for h in range(kv_heads):
        q_buf[me, h] = q_ref[:, h * head_width:(h + 1) * head_width]

    pl.semaphore_wait(barrier, has_left.astype(jnp.int32) + has_right.astype(jnp.int32) + len(peers))
    rows_copy().start()

    def pass_query(s, h):
        @pl.when((s <= me) & has_right)
        def _():
            q_copy(s, h, 0).start()

        @pl.when((s >= me) & has_left)
        def _():
            q_copy(s, h, 1).start()

    for h in range(kv_heads):
        pass_query(me, h)

    lane = lax.broadcasted_iota(jnp.int32, (tokens, entries), 1)

    def softmax_block(scores, values):
        top = jnp.max(scores, axis=1, keepdims=True)
        weights = jnp.exp2((scores - top) * SCORE_FACTOR).astype(jnp.bfloat16)
        return top, jnp.dot(weights, values, preferred_element_type=jnp.float32)

    def compute(s, h):
        columns = pl.ds(pl.multiple_of(h * entries, entries), entries)

        def listed(r):
            entry = table[s, r]
            place = jnp.maximum(entry - 1, 0)
            seen = lengths[s] - lax.rem(place, list_len) * page_len
            return lax.div(place, list_len), jnp.where(entry > 0, seen, 0)

        first, first_seen = listed(0)
        spare = pages[first, 0, 0:8, columns].astype(jnp.float32)[0:1]
        row = lax.broadcasted_iota(jnp.int32, (page_len, entries), 0)

        def lay(r, unused):
            slot, seen_rows = listed(r)
            seen = row < seen_rows
            place = pl.ds(pl.multiple_of(r * page_len, page_len), page_len)
            key = pages[slot, 0, :, columns].astype(jnp.float32)
            value = pages[slot, 1, :, columns].astype(jnp.float32)
            k_buf[place, :] = jnp.where(seen, key, spare).astype(jnp.bfloat16)
            v_buf[place, 0:entries] = jnp.where(seen, value, 0.0).astype(jnp.bfloat16)
            v_buf[place, entries:2 * entries] = jnp.where(seen, 1.0, 0.0).astype(jnp.bfloat16)
            return unused

        lax.fori_loop(0, capacity, lay, 0)
        some = first_seen > 0
        stat = jnp.zeros((tokens, entries), jnp.float32)

        def score(block):
            pair = q_buf[s, h, :, block * 2 * entries:(block + 1) * 2 * entries]
            rows = jnp.concatenate([pair[:, :entries], pair[:, entries:]], axis=0)
            return lax.dot_general(
                rows, k_buf[...], (((1,), (1,)), ((), ())), preferred_element_type=jnp.float32
            )

        blocks = group_heads // 2
        upcoming = score(0)
        for block in range(blocks):
            at = block * 2 * entries
            scores = upcoming
            if block + 1 < blocks:
                upcoming = score(block + 1)
            top, both = softmax_block(scores, v_buf[...])
            weight_sum = both[:, entries:]
            mean = (both[:, :entries] / jnp.maximum(weight_sum, 1.0)).astype(jnp.bfloat16)
            top = jnp.where(some, top, NEG_FILL)
            for k in range(2):
                part[s, h, :, at + k * entries:at + (k + 1) * entries] = mean[k * tokens:(k + 1) * tokens]
                head = 2 * block + k
                stat = jnp.where(lane == head, top[k * tokens:(k + 1) * tokens], stat)
                stat = jnp.where(lane == group_heads + head, weight_sum[k * tokens:(k + 1) * tokens], stat)
        part_stat[s, h] = stat.T[0:2 * group_heads]

    def unit(s, h):
        compute(s, h)

        @pl.when((s > me) & jnp.logical_not(has_left))
        def _():
            for copy in part_copies(s, h, 0):
                copy.start()

        @pl.when((s < me) & jnp.logical_not(has_right))
        def _():
            for copy in part_copies(s, h, 1):
                copy.start()

    def own(h, unused):
        compute(me, h)
        return unused

    page_load.wait()
    lax.fori_loop(0, 1, own, 0)

    rows_in[rep_id] = hidden[:, pl.ds(pl.multiple_of(rep_id * depth, entries), depth)]
    rows_copy().wait_recv()
    weight_load.wait()
    all_rows = rows_in[...].reshape(2 * tokens, depth)
    block_width = 2 * kv_heads * entries
    for t in range(tensors):
        product = jnp.dot(
            all_rows, weight[:, t * block_width:(t + 1) * block_width],
            preferred_element_type=jnp.float32,
        ).astype(jnp.bfloat16)
        for r in range(2):
            products[t, r] = product[r * tokens:(r + 1) * tokens]
    for k in range(len(peers)):
        term_copy(k).start()

    def pass_kv(s):
        @pl.when((s <= me) & has_right)
        def _():
            kv_copy(s, 0).start()

        @pl.when((s >= me) & has_left)
        def _():
            kv_copy(s, 1).start()

    def own_pages():
        total_kv = products[tensor_id, rep_id].astype(jnp.float32)
        for k in range(len(peers)):
            term_copy(k).wait_recv()
            total_kv = total_kv + terms[k].astype(jnp.float32)
        total_kv = total_kv.astype(jnp.bfloat16)
        for head in range(kv_heads):
            for kind in range(2):
                at = (2 * head + kind) * entries
                kv_buf[me, kind, :, head * entries:(head + 1) * entries] = total_kv[:, at:at + entries]
        other_copy().start()
        pass_kv(me)

    def relay_kv(distance):
        for s, inside in ((me - distance, me >= distance), (me + distance, me + distance < stores)):
            @pl.when(inside)
            def _():
                kv_copy(s, 0).wait_recv()
                pass_kv(s)

    def outward(index, unused):
        distance = 1 + index // kv_heads
        h = index % kv_heads
        for s, inside in ((me - distance, me >= distance), (me + distance, me + distance < stores)):
            @pl.when(inside)
            def _():
                q_copy(s, h, 0).wait_recv()
                pass_query(s, h)

        def each(turn, unused):
            s = me + (2 * turn - 1) * distance

            @pl.when((s >= 0) & (s < stores))
            def _():
                unit(s, h)

            return unused

        unused = lax.fori_loop(0, 2, each, unused)
        pl.when(index == 0)(own_pages)

        @pl.when((h == kv_heads - 1) & (distance > 1))
        def _():
            relay_kv(distance - 1)

        return unused

    lax.fori_loop(0, (stores - 1) * kv_heads, outward, 0)
    other_copy().wait_recv()
    at_end = jnp.logical_not(has_left & has_right)
    lax.fori_loop(jnp.where(at_end, 1, kv_heads), kv_heads, own, 0)

    def take_in(s, h, side):
        for copy in part_copies(s, h, side):
            copy.wait_recv()
        mine = part_stat[s, h].T
        theirs = inc_stat[side, s, h].T
        stat = jnp.zeros((tokens, entries), jnp.float32)
        for head in range(group_heads):
            columns = slice(head * entries, (head + 1) * entries)

            def state(where, numbers):
                return (
                    where[:, columns].astype(jnp.float32),
                    jnp.broadcast_to(numbers[:, head:head + 1], (tokens, entries)),
                    jnp.broadcast_to(numbers[:, group_heads + head:group_heads + head + 1], (tokens, entries)),
                )

            mean, top, total = merge(state(part.at[s, h], mine), state(inc.at[side, s, h], theirs))
            part[s, h, :, columns] = mean.astype(jnp.bfloat16)
            stat = jnp.where(lane == head, top, stat)
            stat = jnp.where(lane == group_heads + head, total, stat)
        part_stat[s, h] = stat.T[0:2 * group_heads]

    key_index = lax.broadcasted_iota(jnp.int32, (2 * tokens, 2 * tokens), 1)
    query_index = lax.broadcasted_iota(jnp.int32, (2 * tokens, 2 * tokens), 0) % tokens
    allowed = (key_index - tokens <= query_index) & (key_index >= (1 - rep_id) * tokens)

    def fresh(h, unused):
        columns = pl.ds(pl.multiple_of(h * entries, entries), entries)
        key = jnp.concatenate([other_kv[0, :, columns], kv_buf[me, 0, :, columns]], axis=0)
        value = jnp.concatenate([other_kv[1, :, columns], kv_buf[me, 1, :, columns]], axis=0)
        value = jnp.concatenate([value, jnp.ones((2 * tokens, entries), jnp.bfloat16)], axis=1)
        mine = part_stat[me, h].T
        stat = jnp.zeros((tokens, entries), jnp.float32)
        for block in range(group_heads // 2):
            at = block * 2 * entries
            pair = q_buf[me, h, :, at:at + 2 * entries]
            rows = jnp.concatenate([pair[:, :entries], pair[:, entries:]], axis=0)
            scores = lax.dot_general(
                rows, key, (((1,), (1,)), ((), ())), preferred_element_type=jnp.float32
            )
            top, both = softmax_block(jnp.where(allowed, scores, NEG_FILL), value)
            for k in range(2):
                head = 2 * block + k
                columns_k = slice(at + k * entries, at + (k + 1) * entries)
                span = slice(k * tokens, (k + 1) * tokens)
                total = both[span, entries:]
                mean, peak, total = merge(
                    (both[span, :entries] / total, jnp.broadcast_to(top[span], (tokens, entries)), total),
                    (
                        part[me, h, :, columns_k].astype(jnp.float32),
                        jnp.broadcast_to(mine[:, head:head + 1], (tokens, entries)),
                        jnp.broadcast_to(mine[:, group_heads + head:group_heads + head + 1], (tokens, entries)),
                    ),
                )
                part[me, h, :, columns_k] = mean.astype(jnp.bfloat16)
                stat = jnp.where(lane == head, peak, stat)
                stat = jnp.where(lane == group_heads + head, total, stat)
        part_stat[me, h] = stat.T[0:2 * group_heads]
        return unused

    def inward(index, unused):
        distance = stores - 1 - index // kv_heads
        h = index % kv_heads

        @pl.when((me + distance < stores) & has_left)
        def _():
            take_in(me + distance, h, 0)
            for copy in part_copies(me + distance, h, 0):
                copy.start()

        @pl.when((me >= distance) & has_right)
        def _():
            take_in(me - distance, h, 1)
            for copy in part_copies(me - distance, h, 1):
                copy.start()

        return unused

    lax.fori_loop(0, (stores - 1) * kv_heads, inward, 0)
    lax.fori_loop(jnp.where(at_end, kv_heads, 1), kv_heads, own, 0)
    lax.fori_loop(0, kv_heads, fresh, 0)

    def finish(h, unused):
        @pl.when(has_left)
        def _():
            take_in(me, h, 0)

        @pl.when(has_right)
        def _():
            take_in(me, h, 1)

        width = pl.ds(pl.multiple_of(h * head_width, head_width), head_width)
        out_ref[:, width] = part[me, h]
        return unused

    relay_kv(stores - 1)
    source = 0
    for s in range(1, stores):
        source = jnp.where(new_owner[rep_id, s] == me, s, source)
    added_ref[...] = kv_buf[source]
    lax.fori_loop(0, kv_heads, finish, 0)
    rows_copy().wait_send()
    for k in range(len(peers)):
        term_copy(k).wait_send()
    other_copy().wait_send()

    def drain_kv(s, unused):
        @pl.when((s <= me) & has_right)
        def _():
            kv_copy(s, 0).wait_send()

        @pl.when((s >= me) & has_left)
        def _():
            kv_copy(s, 1).wait_send()

        return unused

    lax.fori_loop(0, stores, drain_kv, 0)

    def drain(index, unused):
        s = index // kv_heads
        h = index % kv_heads

        @pl.when((s <= me) & has_right)
        def _():
            q_copy(s, h, 0).wait_send()

        @pl.when((s >= me) & has_left)
        def _():
            q_copy(s, h, 1).wait_send()

        @pl.when(s != me)
        def _():
            for copy in part_copies(s, h, 0):
                copy.wait_send()

        return unused

    lax.fori_loop(0, stores * kv_heads, drain, 0)


def buffers_of(stores, tensors, kv_heads, group_heads, capacity, tokens, page_len, weight, page_store):
    head_width = group_heads * HEAD_ENTRIES
    stat_rows = 2 * group_heads
    block_width = 2 * kv_heads * HEAD_ENTRIES
    return [
        pltpu.VMEM((stores, kv_heads, tokens, head_width), jnp.bfloat16),
        pltpu.VMEM((stores, kv_heads, tokens, head_width), jnp.bfloat16),
        pltpu.VMEM((stores, kv_heads, stat_rows, tokens), jnp.float32),
        pltpu.VMEM((2, stores, kv_heads, tokens, head_width), jnp.bfloat16),
        pltpu.VMEM((2, stores, kv_heads, stat_rows, tokens), jnp.float32),
        pltpu.VMEM((capacity * page_len, HEAD_ENTRIES), jnp.bfloat16),
        pltpu.VMEM((capacity * page_len, 2 * HEAD_ENTRIES), jnp.bfloat16),
        pltpu.VMEM(weight.shape, weight.dtype),
        pltpu.VMEM(page_store.shape, page_store.dtype),
        pltpu.VMEM((2, tokens, weight.shape[0]), jnp.bfloat16),
        pltpu.VMEM((tensors, 2, tokens, block_width), jnp.bfloat16),
        pltpu.VMEM((2 * tensors - 1, tokens, block_width), jnp.bfloat16),
        pltpu.VMEM((stores, 2, tokens, block_width // 2), jnp.bfloat16),
        pltpu.VMEM((2, tokens, block_width // 2), jnp.bfloat16),
        pltpu.SemaphoreType.DMA((2, stores, kv_heads)),
        pltpu.SemaphoreType.DMA((stores, kv_heads)),
        pltpu.SemaphoreType.DMA((stores, kv_heads)),
        pltpu.SemaphoreType.DMA((2, stores, kv_heads)),
        pltpu.SemaphoreType.DMA((stores, kv_heads)),
        pltpu.SemaphoreType.DMA((2, stores, kv_heads)),
        pltpu.SemaphoreType.DMA((2,)),
        pltpu.SemaphoreType.DMA,
        pltpu.SemaphoreType.DMA,
        pltpu.SemaphoreType.DMA((2 * tensors - 1,)),
        pltpu.SemaphoreType.DMA((2 * tensors - 1,)),
        pltpu.SemaphoreType.DMA((2, stores)),
        pltpu.SemaphoreType.DMA((stores,)),
        pltpu.SemaphoreType.DMA,
        pltpu.SemaphoreType.DMA,
    ]


def attend(
    table, lengths, new_owner, own_queries, own_rows, weight, page_store,
    list_len, stores, tensors, kv_heads,
):
    tokens = own_queries.shape[0]
    page_len = page_store.shape[2]
    group_heads = own_queries.shape[1] // (kv_heads * HEAD_ENTRIES)
    capacity = table.shape[1]
    sizes = (stores, tensors, kv_heads, group_heads, capacity, tokens, page_len)
    smem = pl.BlockSpec(memory_space=pltpu.SMEM)
    vmem = pl.BlockSpec(memory_space=pltpu.VMEM)
    where_it_is = pl.BlockSpec(memory_space=pl.ANY)
    pairs = stores * capacity * page_len * tokens * kv_heads * group_heads
    return pl.pallas_call(
        functools.partial(attend_kernel, list_len, *sizes),
        out_shape=(
            jax.ShapeDtypeStruct(own_queries.shape, jnp.bfloat16),
            jax.ShapeDtypeStruct((2, tokens, kv_heads * HEAD_ENTRIES), jnp.bfloat16),
        ),
        in_specs=[smem, smem, smem, vmem, vmem, where_it_is, where_it_is],
        out_specs=(vmem, vmem),
        scratch_shapes=buffers_of(*sizes, weight, page_store),
        compiler_params=pltpu.CompilerParams(
            collective_id=0, has_side_effects=True, vmem_limit_bytes=KERNEL_BYTES
        ),
        cost_estimate=pl.CostEstimate(
            flops=4 * pairs * HEAD_ENTRIES, bytes_accessed=2 * page_store.size, transcendentals=pairs
        ),
        name="attend_pages",
    )(table, lengths, new_owner, own_queries, own_rows, weight, page_store)


def push_shards(
    queries, hidden, key_value_weight, page_store, prefix_holder, prefix_slot, prefix_len, new_owner
):
    store_id = lax.axis_index("store")
    stores = lax.axis_size("store")
    tensors = lax.axis_size("tensor")
    kv_heads = page_store.shape[3] // HEAD_ENTRIES
    list_len = prefix_slot.shape[1]
    capacity = 2 * max(2, list_len // (2 * stores))
    table = held_table(prefix_holder[:, :, 0], prefix_slot, capacity, store_id)
    attended, added = attend(
        table, prefix_len, new_owner, queries[0], hidden[0], key_value_weight, page_store,
        list_len, stores, tensors, kv_heads,
    )
    return (attended[None], added[None, None])


def held_in_vmem(mesh, queries, page_store):
    stores = mesh.shape["store"]
    page_bytes = 2 * page_store.size // (mesh.shape["group"] * stores * mesh.shape["tensor"])
    query_bytes = 2 * queries.size // (mesh.shape["group"] * mesh.shape["tensor"] * mesh.shape["rep"])
    return page_bytes + 4 * query_bytes < KERNEL_BYTES // 2


def solution(mesh):
    placed = (
        P(("group", "store"), "rep", "tensor"),
        P(("group", "store"), "rep", "tensor"),
        P(("tensor", "rep"), None),
        P(("group", "store"), None, None, "tensor"),
        P("group", None, None),
        P("group", None),
        P("group"),
        P(None, "group"),
    )
    build = functools.partial(
        jax.shard_map,
        mesh=mesh,
        in_specs=placed,
        out_specs=(
            P(("group", "store"), "rep", "tensor"),
            P(("group", "store"), "rep", None, None, "tensor"),
        ),
        check_vma=False,
    )

    def whole(*arrays):
        fits = held_in_vmem(mesh, arrays[0], arrays[3])
        return build(push_shards if fits else pull_shards)(*arrays)

    return whole
```
